128 devices in a mesh: slab: 16 (over x, y), cross: 8 (over z, core).
Axes of the slice: x: 4, y: 4, z: 4, core: 2. Of those that a mesh axis runs over, the one named last changes fastest.
Arguments:
- rhs: float32 [64, 64, 32, 128], P(None, 'slab', 'cross'), may hold values from -6 to 6
- classes: int32 [64, 32, 128], P('slab', 'cross'), may hold values from 0 to 15
- perm: float32 [16], replicated, may hold values from 0.1 to 10
- vol_block: float32 [64, 64], replicated, may hold values from -0.72 to 3.5
- side_blocks: float32 [6, 64, 64], replicated, may hold values from -0.24 to 1.3
- couple: float32 [3, 64, 64], replicated, may hold values from -0.24 to 0.5
- smoother_blocks: float32 [16, 64, 64], replicated, may hold values from -0.024 to 0.09
- restrict_map: float32 [8, 64], replicated, may hold values from -0.75 to 0.75
- coarse_block: float32 [8, 8], replicated, may hold values from -0.048 to 0.09
- owners: int32 [16, 8, 2048, 1], P('slab', 'cross'), may hold values from 0 to 127, as said below
- agg_local: int32 [16, 8, 2048], P('slab', 'cross'), may hold values from 0 to 127
Outputs:
- solution: float32 [64, 64, 32, 128], P(None, 'slab', 'cross')
- residual: float32 [64, 64, 32, 128], P(None, 'slab', 'cross')
The draws below stay inside these ranges and needn't reach their ends.
Inputs may be any that keep to these rules, and one draw needn't show every extreme that they name: `owners`: no owner is named by more than 32 of one device's elements, and some owner is named by exactly 32 elements of some device.
All inputs are finite; a program needn't handle non-finite values.
Results may differ from the reference program's by a relative error of at most 0.0003.
Values sent between devices are 32-bit elements; how exact they have to be, the bound alone decides.
A program may use at most 128 MiB of HBM per device.

```python
import math
import jax
import jax.numpy as jnp
from jax import lax

NODES = 64
CLASSES = 16
CW = 8
EX = 4
EY = 4
ELEMS = 2048
CAP = 32
AGG_DEV = 128
NX = 64
NY = 32
NZ = 128
N_SLAB = 16
N_CROSS = 8
DEVICES = 128


def dominant(key, count, order, low, high, spread):
    first, second = jax.random.split(key)
    diagonal = jax.random.uniform(first, (count, order), jnp.float32, low, high)
    scatter = jnp.clip(jax.random.normal(second, (count, order, order), jnp.float32), -6.0, 6.0) * spread
    identity = (jnp.arange(order)[:, None] == jnp.arange(order)[None, :]).astype(jnp.float32)
    return scatter * (1.0 - identity) + identity * diagonal[:, :, None]


def agglomerate_layout(key):
    run_length = min(CAP, 32)
    per_owner = CAP // run_length
    run_total = ELEMS // run_length
    busy_count = DEVICES // 8
    rank_key, pick_key, index_key, mixing_key = jax.random.split(key, 4)
    ranking = jax.random.permutation(rank_key, DEVICES).astype(jnp.int32)
    busy_slots = jnp.repeat(ranking[:busy_count], per_owner)
    other_slots = jnp.repeat(ranking[busy_count:], per_owner)
    other_needed = run_total - busy_count * per_owner

    def one_device(device_key):
        first, second = jax.random.split(device_key)
        picked = jax.random.permutation(first, other_slots)[:other_needed]
        return jax.random.permutation(second, jnp.concatenate([busy_slots, picked]))
    run_owner = jax.vmap(one_device)(jax.random.split(pick_key, DEVICES)).astype(jnp.int32)
    run_index = jax.random.randint(index_key, (DEVICES, run_total), 0, AGG_DEV, dtype=jnp.int32)
    run_index = run_index.at[0, 0].set(AGG_DEV - 1).at[0, 1].set(0)
    owner_elem = jnp.repeat(run_owner, run_length, axis=1)
    index_elem = jnp.repeat(run_index, run_length, axis=1)
    mixing = jax.random.permutation(mixing_key, ELEMS)
    owner_elem = owner_elem.at[DEVICES - 1].set(owner_elem[DEVICES - 1][mixing])
    index_elem = index_elem.at[DEVICES - 1].set(index_elem[DEVICES - 1][mixing])
    return (owner_elem.reshape(N_SLAB, N_CROSS, ELEMS, 1), index_elem.reshape(N_SLAB, N_CROSS, ELEMS))


def draw_vol_block(key, part):
    key = jax.random.fold_in(key, 1)
    return dominant(key, 1, NODES, 2.5, 3.5, 0.12)[0]


def draw_side_blocks(key, part):
    key = jax.random.fold_in(key, 2)
    return dominant(key, 6, NODES, 0.7, 1.3, 0.04)


def draw_smoother_blocks(key, part):
    key = jax.random.fold_in(key, 3)
    return dominant(key, CLASSES, NODES, 0.05, 0.09, 0.004)


def draw_coarse_block(key, part):
    key = jax.random.fold_in(key, 4)
    return dominant(key, 1, CW, 0.05, 0.09, 0.008)[0]


def draw_couple(key, part):
    key = jax.random.fold_in(key, 6)
    return dominant(key, 3, NODES, 0.3, 0.5, 0.04)


def draw_owners(key, part):
    shared = agglomerate_layout(key)
    return shared[0]


def draw_agg_local(key, part):
    shared = agglomerate_layout(key)
    return shared[1]


def touch_ends(values, key, smallest, top_value):
    place = [jax.random.randint(jax.random.fold_in(key, axis), (), 0, length) for axis, length in enumerate(values.shape)]
    longest = values.shape.index(max(values.shape))
    beside = place[:longest] + [(place[longest] + 1) % values.shape[longest]] + place[longest + 1:]
    return values.at[tuple(place)].set(smallest).at[tuple(beside)].set(top_value)


def level_of(rng, extent, shards, low, largest):
    loudness, own = 1.0, jax.random.fold_in(rng, 6)
    for dim, parts in shards:
        heights = jnp.exp(jax.random.uniform(jax.random.fold_in(own, dim), (parts,), jnp.float32, low / len(shards), largest / len(shards)))
        loudness = loudness * jnp.repeat(heights, extent[dim] // parts).reshape([-1 if axis == dim else 1 for axis in range(len(extent))])
    return loudness


def bell_draw(stream_key, shape, scale, bound, cuts=(), kind=jnp.bfloat16):
    values = scale * jax.random.normal(stream_key, shape, jnp.float32)
    if cuts:
        values = values * level_of(stream_key, shape, cuts, -0.22, 0.18)
    return jnp.clip(values, -bound, bound).astype(kind)


def setup_inputs(seed: int = 0) -> dict:
    streams_of = jax.random.split(jax.random.key(seed), 12)
    return {
        "rhs": bell_draw(streams_of[0], (NODES, NX, NY, NZ), 1.0, 6.0, ((1, 16), (2, 8)), jnp.float32),
        "classes": touch_ends(jax.random.randint(streams_of[1], (NX, NY, NZ), 0, CLASSES), jax.random.fold_in(streams_of[1], 1), 0, CLASSES - 1).astype(jnp.int32),
        "perm": jnp.clip(jnp.exp(jax.random.uniform(streams_of[2], (CLASSES,), jnp.float32, math.log(0.1), math.log(10.0))), 0.1, 10.0),
        "vol_block": draw_vol_block(jax.random.fold_in(streams_of[11], 71), 0),
        "side_blocks": draw_side_blocks(jax.random.fold_in(streams_of[11], 71), 0),
        "couple": draw_couple(jax.random.fold_in(streams_of[11], 71), 0),
        "smoother_blocks": draw_smoother_blocks(jax.random.fold_in(streams_of[11], 71), 0),
        "restrict_map": bell_draw(streams_of[7], (CW, NODES), NODES ** -0.5, 0.75, (), jnp.float32),
        "coarse_block": draw_coarse_block(jax.random.fold_in(streams_of[11], 71), 0),
        "owners": draw_owners(jax.random.fold_in(streams_of[11], 71), 0),
        "agg_local": draw_agg_local(jax.random.fold_in(streams_of[11], 71), 0),
    }


def apply_block(matrix, field):
    return jnp.einsum('ij,jabc->iabc', matrix, field, precision=lax.Precision.HIGHEST)


def neighbours(padded):
    return [padded[..., :-2, 1:-1, 1:-1], padded[..., 2:, 1:-1, 1:-1],
            padded[..., 1:-1, :-2, 1:-1], padded[..., 1:-1, 2:, 1:-1],
            padded[..., 1:-1, 1:-1, :-2], padded[..., 1:-1, 1:-1, 2:]]


def cell_perm(classes, perm):
    labels = jnp.arange(perm.shape[0], dtype=jnp.int32)[:, None, None, None]
    return jnp.sum(jnp.where(classes[None] == labels, perm[:, None, None, None], 0.0), axis=0)


def face_weights(perm_cell, padded_perm):
    result = []
    for other in neighbours(padded_perm):
        result.append(jnp.where(other > 0.0, 2.0 * perm_cell * other / (perm_cell + other), 2.0 * perm_cell))
    return result


def operate(field, padded_field, perm_cell, weights, vol_block, side_blocks, couple):
    result = perm_cell * apply_block(vol_block, field)
    others = neighbours(padded_field)
    for direction in range(6):
        coupling = couple[direction // 2]
        if direction % 2 == 0:
            coupling = coupling.T
        result = result + weights[direction] * (apply_block(side_blocks[direction], field) - apply_block(coupling, others[direction]))
    return result


def smooth(iterate, residue, classes, perm_cell, smoother_blocks):
    node_count = residue.shape[0]
    group_rows = ELEMS
    grouped = residue.reshape(node_count, -1, group_rows).transpose(1, 0, 2)
    labels = classes.reshape(-1, group_rows).astype(jnp.int32)

    def one_group(pieces):
        values, label_row = pieces
        blocks = smoother_blocks[label_row]
        return jnp.einsum('eij,je->ie', blocks, values, precision=lax.Precision.HIGHEST)

    applied = lax.map(one_group, (grouped, labels))
    update = applied.transpose(1, 0, 2).reshape(residue.shape)
    return iterate + update / perm_cell


def reference(rhs, classes, perm, vol_block, side_blocks, couple, smoother_blocks, restrict_map, coarse_block, owners, agg_local):
    perm_cell = cell_perm(classes, perm)
    weights = face_weights(perm_cell, jnp.pad(perm_cell, 1))

    def fine_op(field):
        padded = jnp.pad(field, ((0, 0), (1, 1), (1, 1), (1, 1)))
        return operate(field, padded, perm_cell, weights, vol_block, side_blocks, couple)

    def sweep(iterate):
        return smooth(iterate, rhs - fine_op(iterate), classes, perm_cell, smoother_blocks)

    def to_elements(field):
        leading = field.shape[0]
        shaped = field.reshape(leading, N_SLAB, EX, N_CROSS, EY, NZ)
        return shaped.transpose(0, 1, 3, 2, 4, 5).reshape(leading, -1)

    def from_elements(values):
        leading = values.shape[0]
        shaped = values.reshape(leading, N_SLAB, N_CROSS, EX, EY, NZ)
        return shaped.transpose(0, 1, 3, 2, 4, 5).reshape(leading, NX, NY, NZ)

    target = (owners.reshape(-1) * AGG_DEV + agg_local.reshape(-1)).astype(jnp.int32)
    total_coarse = AGG_DEV * N_SLAB * N_CROSS

    def restrict(field):
        fine = jnp.dot(restrict_map, to_elements(field), precision=lax.Precision.HIGHEST)
        return jax.ops.segment_sum(fine.T, target, total_coarse).T

    def prolong(coarse):
        return from_elements(jnp.dot(restrict_map.T, coarse[:, target], precision=lax.Precision.HIGHEST))

    perm_sum = jax.ops.segment_sum(to_elements(perm_cell[None])[0], target, total_coarse)
    coarse_scale = 1.0 / (1.0 + perm_sum)

    iterate = smooth(jnp.zeros_like(rhs), rhs, classes, perm_cell, smoother_blocks)
    iterate = sweep(iterate)
    fine_res = rhs - fine_op(iterate)
    coarse_res = restrict(fine_res)
    first = coarse_scale * jnp.dot(coarse_block, coarse_res, precision=lax.Precision.HIGHEST)
    again = coarse_res - restrict(fine_op(prolong(first)))
    second = first + coarse_scale * jnp.dot(coarse_block, again, precision=lax.Precision.HIGHEST)
    iterate = iterate + prolong(second)
    iterate = sweep(iterate)
    iterate = sweep(iterate)
    return iterate, rhs - fine_op(iterate)
```

```python
import functools

import jax
import jax.numpy as jnp
from jax import lax
from jax.experimental import pallas as pl
from jax.experimental.pallas import tpu as pltpu
from jax.sharding import PartitionSpec as P

MESH = pl.DeviceIdType.MESH
F32 = jnp.float32
BF16 = jnp.bfloat16
HIGHEST = lax.Precision.HIGHEST
LANES = 128
WIDE = 4
NT = (((1,), (1,)), ((), ()))


def dot(a, b):
    return jnp.dot(a, b, preferred_element_type=F32)


def dot_nt(a, b):
    return lax.dot_general(a, b, NT, preferred_element_type=F32)


def parts(value):
    high = value.astype(BF16).astype(F32)
    return high, value - high


def stack_rows(value):
    high, low = parts(value)
    pieces = [high, low, high]
    if value.shape[0] == 8:
        pieces.append(jnp.zeros_like(value))
    return jnp.concatenate(pieces, axis=0).astype(BF16)


def stack_columns(value):
    high, low = parts(value)
    pieces = [high, high, low]
    if value.shape[1] == 8:
        pieces.append(jnp.zeros_like(value))
    return jnp.concatenate(pieces, axis=1).astype(BF16)


def cycle(
    n_slab,
    n_cross,
    cap,
    rhs_ref,
    class_ref,
    perm_ref,
    vol_ref,
    side_ref,
    couple_ref,
    smooth_ref,
    restrict_ref,
    coarse_ref,
    owner_ref,
    local_ref,
    sol_ref,
    res_ref,
    rs,
    halo_rhs,
    fields,
    halos,
    start_field,
    fine_res,
    acc,
    gx0,
    gx1,
    gy0,
    gy1,
    blocks_f32,
    op_stack,
    smooth_stack,
    prolong_stack,
    coarse_stack,
    perm_b,
    perm_inv,
    weights,
    owner_hot,
    rank_b,
    packed,
    local_hot,
    mail,
    coarse_keep,
    coarse_field,
    halo_coarse,
    halo_send,
    halo_recv,
    mail_send,
    mail_recv,
):
    s, c = lax.axis_index("slab"), lax.axis_index("cross")
    owners = n_slab * n_cross
    s_up, s_down = lax.rem(s + 1, n_slab), lax.rem(s + n_slab - 1, n_slab)
    c_up, c_down = lax.rem(c + 1, n_cross), lax.rem(c + n_cross - 1, n_cross)
    lane = lax.broadcasted_iota(jnp.int32, (8, LANES), 1)

    barrier = pltpu.get_barrier_semaphore()

    def greet_slab(off, carry):
        pl.semaphore_signal(
            barrier, inc=1, device_id=(lax.rem(s + off, n_slab), c), device_id_type=MESH
        )
        return carry

    def greet_cross(off, carry):
        pl.semaphore_signal(
            barrier, inc=1, device_id=(s, lax.rem(c + off, n_cross)), device_id_type=MESH
        )
        return carry

    lax.fori_loop(1, n_slab, greet_slab, 0)
    lax.fori_loop(1, n_cross, greet_cross, 0)

    for xy in range(WIDE * WIDE):
        x, y = xy // WIDE, xy % WIDE
        rs[x, y, 0:64, :] = rhs_ref[pl.ds(xy, 64, stride=WIDE * WIDE), :]
        rs[x, y, 64:72, :] = jnp.broadcast_to(class_ref[xy : xy + 1, :], (8, LANES)).astype(F32)

    pl.semaphore_wait(barrier, n_slab + n_cross - 2)

    def halo_copies(source, target, turn):
        plan = (
            (source.at[0], 1, (s_down, c)),
            (source.at[WIDE - 1], 0, (s_up, c)),
            (source.at[:, 0], 3, (s, c_down)),
            (source.at[:, WIDE - 1], 2, (s, c_up)),
        )
        return [
            pltpu.make_async_remote_copy(
                src_ref=face,
                dst_ref=target.at[side],
                send_sem=halo_send.at[turn, side],
                recv_sem=halo_recv.at[turn, side],
                device_id=device,
                device_id_type=MESH,
            )
            for face, side, device in plan
        ]

    def send_halo(source, target, turn):
        for copy in halo_copies(source, target, turn):
            copy.start()

    def await_halo(source, target, turn):
        for copy in halo_copies(source, target, turn):
            copy.wait_recv()

    send_halo(rs, halo_rhs, 0)

    blocks_f32[0:64, :] = vol_ref[...]
    blocks_f32[64:448, :] = side_ref[...]
    for m in range(3):
        plus = couple_ref[m * 64 : (m + 1) * 64, :]
        blocks_f32[448 + 128 * m : 512 + 128 * m, :] = plus.T
        blocks_f32[512 + 128 * m : 576 + 128 * m, :] = plus
    blocks_f32[832:896, :] = jnp.where(
        lax.broadcasted_iota(jnp.int32, (64, 64), 0) == lax.broadcasted_iota(jnp.int32, (64, 64), 1),
        1.0,
        0.0,
    )
    for m in range(13):
        rows = slice(64 * m, 64 * m + 64)
        op_stack[rows, :] = stack_columns(blocks_f32[rows, :])
    for m in range(16):
        rows = slice(64 * m, 64 * m + 64)
        smooth_stack[rows, :] = stack_columns(smooth_ref[rows, :])
    restrict = restrict_ref[...]
    short = lax.dot_general(
        blocks_f32[...], restrict, NT, precision=HIGHEST, preferred_element_type=F32
    )
    prolong_stack[...] = stack_columns(short)
    tiny = [
        jnp.dot(restrict, short[64 * m : 64 * m + 64], precision=HIGHEST, preferred_element_type=F32)
        for m in range(13)
    ]
    coarse_stack[...] = stack_columns(jnp.concatenate(tiny + [jnp.zeros((8, 8), F32)], axis=0))
    restrict_cols = stack_columns(jnp.concatenate([restrict, jnp.zeros_like(restrict)], axis=0))

    hot_rows = lax.broadcasted_iota(jnp.int32, (owners, LANES), 0)
    before = jnp.concatenate(
        [
            jnp.where(
                lax.broadcasted_iota(jnp.int32, (LANES, LANES), 0)
                < lax.broadcasted_iota(jnp.int32, (LANES, LANES), 1),
                1.0,
                0.0,
            ),
            jnp.ones((LANES, LANES), F32),
        ],
        axis=1,
    ).astype(BF16)
    seen = jnp.zeros((owners, LANES), F32)
    for xy in range(WIDE * WIDE):
        x, y = xy // WIDE, xy % WIDE
        hot = jnp.where(hot_rows == owner_ref[xy : xy + 1, :], 1.0, 0.0)
        hot_low = hot.astype(BF16)
        owner_hot[0:owners, xy * LANES : (xy + 1) * LANES] = hot_low
        owner_hot[owners : 2 * owners, xy * LANES : (xy + 1) * LANES] = hot_low
        counted = dot(hot_low, before)
        rank = jnp.sum(hot * (counted[:, 0:LANES] + seen), axis=0, keepdims=True)
        seen = seen + counted[:, LANES : 2 * LANES]
        rank_b[x, y] = jnp.broadcast_to(rank, (8, LANES))

    def perm_of(label):
        value = jnp.zeros_like(label)
        for k in range(16):
            value = jnp.where(label == float(k), perm_ref[k], value)
        return value

    def own_perm(x, carry):
        for y in range(WIDE):
            value = perm_of(rs[x, y, 64:72, :])
            perm_b[x, y] = value
            perm_inv[x, y] = 1.0 / value
        return carry

    lax.fori_loop(0, WIDE, own_perm, 0)

    def slab_copy(turn, source, target, off, stage):
        to = lax.rem(s + off, n_slab)
        return pltpu.make_async_remote_copy(
            src_ref=mail.at[turn, source, :, pl.ds(pl.multiple_of(to * n_cross, n_cross), n_cross)],
            dst_ref=mail.at[turn, target, :, pl.ds(pl.multiple_of(s * n_cross, n_cross), n_cross)],
            send_sem=mail_send.at[turn, stage],
            recv_sem=mail_recv.at[turn, stage],
            device_id=(to, c),
            device_id_type=MESH,
        )

    def cross_copy(turn, source, target, off, stage):
        to = lax.rem(c + off, n_cross)
        return pltpu.make_async_remote_copy(
            src_ref=mail.at[turn, source, :, pl.ds(pl.multiple_of(to * n_slab, n_slab), n_slab)],
            dst_ref=mail.at[turn, target, :, pl.ds(pl.multiple_of(c * n_slab, n_slab), n_slab)],
            send_sem=mail_send.at[turn, stage],
            recv_sem=mail_recv.at[turn, stage],
            device_id=(s, to),
            device_id_type=MESH,
        )

    def post(turn, source, target, stage, along_slab):
        def one(off, carry):
            (slab_copy if along_slab else cross_copy)(turn, source, target, off, stage).start()
            return carry

        lax.fori_loop(1, n_slab if along_slab else n_cross, one, 0)
        size, place = (n_cross, s) if along_slab else (n_slab, c)
        rows = pl.ds(pl.multiple_of(place * size, size), size)
        mail[turn, target, :, rows, :] = mail[turn, source, :, rows, :]

    def rows_moved(along_slab):
        return (n_slab - 1) * n_cross if along_slab else (n_cross - 1) * n_slab

    def collect(turn, target, stage, along_slab):
        part = mail.at[turn, target, :, pl.ds(0, rows_moved(along_slab))]
        pltpu.make_async_copy(part, part, mail_recv.at[turn, stage]).wait()

    def release(turn, source, stage, along_slab):
        part = mail.at[turn, source, :, pl.ds(0, rows_moved(along_slab))]
        pltpu.make_async_copy(part, part, mail_send.at[turn, stage]).wait()

    def write_mail(turn, value):
        for h in range(cap // 16):
            mail[turn, 0, h] = value[:, h * LANES : (h + 1) * LANES]

    def read_mail(turn):
        return jnp.concatenate([mail[turn, 3, h].T for h in range(cap // 16)], axis=0)

    def pack(load):
        def one(x, carry):
            for y in range(WIDE):
                rank = rank_b[x, y]
                keep = [rank == float(r) for r in range(cap)]
                columns = pl.ds(pl.multiple_of((x * WIDE + y) * LANES, LANES), LANES)
                for i, piece in enumerate(parts(load(x, y))):
                    spread = jnp.concatenate([jnp.where(k, piece, 0.0) for k in keep], axis=0)
                    packed[i * cap * 8 : (i + 1) * cap * 8, columns] = spread.astype(BF16)
            return carry

        lax.fori_loop(0, WIDE, one, 0)

    def to_owner_start(turn, load):
        pack(load)
        slots = dot_nt(owner_hot[0:owners, :], packed[...])
        write_mail(turn, slots[:, 0 : cap * 8] + slots[:, cap * 8 : 2 * cap * 8])
        post(turn, 0, 1, 0, True)

    def to_owner_middle(turn):
        collect(turn, 1, 0, True)
        for k in range(n_cross):
            for h in range(cap // 16):
                mail[turn, 2, h, k * n_slab : (k + 1) * n_slab, :] = mail[
                    turn, 1, h, pl.ds(k, n_slab, stride=n_cross), :
                ]
        post(turn, 2, 3, 1, False)

    def to_owner_end(turn):
        collect(turn, 3, 1, False)
        return read_mail(turn)

    def gather_sum(arrived):
        flat = jnp.concatenate([arrived[8 * r : 8 * r + 8] for r in range(cap)], axis=1)
        high, low = parts(flat)
        both = dot_nt(jnp.concatenate([high, low], axis=0).astype(BF16), local_hot[...])
        return both[0:8] + both[8:16]

    def from_owner_start(turn, value):
        high, low = parts(value)
        both = dot(jnp.concatenate([high, low], axis=0).astype(BF16), local_hot[...])
        flat = both[0:8] + both[8:16]
        out = jnp.concatenate([flat[:, owners * r : owners * (r + 1)] for r in range(cap)], axis=0)
        write_mail(turn, out.T)
        post(turn, 0, 1, 0, False)

    def from_owner_middle(turn):
        collect(turn, 1, 0, False)
        for k in range(n_slab):
            for h in range(cap // 16):
                mail[turn, 2, h, k * n_cross : (k + 1) * n_cross, :] = mail[
                    turn, 1, h, pl.ds(k, n_cross, stride=n_slab), :
                ]
        post(turn, 2, 3, 1, True)

    def from_owner_end(turn, target):
        collect(turn, 3, 1, True)
        high, low = parts(read_mail(turn))
        spread = jnp.concatenate([high, low], axis=1).astype(BF16)
        for pair in range(WIDE * WIDE // 2):
            both = dot(spread, owner_hot[:, pair * 2 * LANES : (pair + 1) * 2 * LANES])
            for i in range(2):
                x, y = (2 * pair + i) // WIDE, (2 * pair + i) % WIDE
                rank = rank_b[x, y]
                value = jnp.zeros((8, LANES), F32)
                for r in range(cap):
                    value = jnp.where(
                        rank == float(r),
                        both[8 * r : 8 * r + 8, i * LANES : (i + 1) * LANES],
                        value,
                    )
                coarse_field[target, x, y] = value

    def own_products(load, stack, rows, extra=None):
        def one(x, carry):
            for half in range(2):
                ys = (2 * half, 2 * half + 1)
                product = dot(stack[...], jnp.concatenate([load(x, y) for y in ys], axis=1))
                for i, y in enumerate(ys):

                    def block(b):
                        return product[b * rows : (b + 1) * rows, i * LANES : (i + 1) * LANES]

                    def scaled(weight, value):
                        return weight[None] * value.reshape(rows // 8, 8, LANES)

                    total = scaled(perm_b[x, y], block(0))
                    for d in range(6):
                        total = total + scaled(weights[d, x, y], block(1 + d))
                    total = total - scaled(weights[10, x, y], pltpu.roll(block(11), 1, 1))
                    total = total - scaled(weights[11, x, y], pltpu.roll(block(12), LANES - 1, 1))
                    acc[x, y, 0:rows, :] = total.reshape(rows, LANES)
                    gx0[x + 1, y, 0:rows, :] = block(7)
                    gx1[x, y, 0:rows, :] = block(8)
                    gy0[x, y + 1, 0:rows, :] = block(9)
                    gy1[x, y, 0:rows, :] = block(10)
                    if extra is not None:
                        extra(x, y, block(13))
            return carry

        lax.fori_loop(0, WIDE, one, 0)

    def halo_products(load, stack, rows):
        for side in range(4):
            data = jnp.concatenate([load(side, j) for j in range(WIDE)], axis=1)
            if rows == 64:
                product = dot(stack[(7 + side) * rows : (8 + side) * rows, :], data)
            else:
                product = dot(stack[...], data)[(7 + side) * rows : (8 + side) * rows]
            for j in range(WIDE):
                value = product[:, j * LANES : (j + 1) * LANES]
                if side == 0:
                    gx0[0, j, 0:rows, :] = value
                elif side == 1:
                    gx1[WIDE, j, 0:rows, :] = value
                elif side == 2:
                    gy0[j, 0, 0:rows, :] = value
                else:
                    gy1[j, WIDE, 0:rows, :] = value

    def applied(x, y, rows):
        def scaled(weight, value):
            return weight[None] * value.reshape(rows // 8, 8, LANES)

        total = acc[x, y, 0:rows, :].reshape(rows // 8, 8, LANES)
        total = total - scaled(weights[6, x, y], gx0[x, y, 0:rows, :])
        total = total - scaled(weights[7, x, y], gx1[x + 1, y, 0:rows, :])
        total = total - scaled(weights[8, x, y], gy0[x, y, 0:rows, :])
        total = total - scaled(weights[9, x, y], gy1[x, y + 1, 0:rows, :])
        return total.reshape(rows, LANES)

    def smoothed(values, labels, inverses):
        product = dot(smooth_stack[...], jnp.concatenate([stack_rows(v) for v in values], axis=1))
        results = []
        for i, (label, inverse) in enumerate(zip(labels, inverses)):
            columns = slice(i * LANES, (i + 1) * LANES)
            value = product[0:64, columns].reshape(8, 8, LANES)
            for k in range(1, 16):
                block = product[64 * k : 64 * k + 64, columns].reshape(8, 8, LANES)
                value = jnp.where((label == float(k))[None], block, value)
            results.append((value * inverse[None]).reshape(64, LANES))
        return results

    def label_of(x, y):
        return rs[x, y, 64:72, :]

    def first_sweep(x, carry):
        for half in range(2):
            ys = (2 * half, 2 * half + 1)
            found = smoothed(
                [rs[x, y, 0:64, :] for y in ys],
                [label_of(x, y) for y in ys],
                [perm_inv[x, y] for y in ys],
            )
            for y, value in zip(ys, found):
                start_field[x, y] = value
        return carry

    lax.fori_loop(0, WIDE, first_sweep, 0)

    def keys(x, y):
        row = lax.broadcasted_iota(jnp.int32, (8, LANES), 0)
        label = jnp.broadcast_to(local_ref[pl.ds(x * WIDE + y, 1), :], (8, LANES)).astype(F32) + 1.0
        return jnp.where(row == 0, label, jnp.where(row == 1, perm_b[x, y], 0.0))

    to_owner_start(0, keys)

    await_halo(rs, halo_rhs, 0)
    inside = (s > 0, s < n_slab - 1, c > 0, c < n_cross - 1)

    def halo_sweep(side, carry):
        label = [halo_rhs[side, j, 64:72, :] for j in range(WIDE)]
        found = [perm_of(v) for v in label]
        for j in range(WIDE):
            halo_coarse[0, side, j] = found[j]
        for half in range(2):
            js = (2 * half, 2 * half + 1)
            values = smoothed(
                [halo_rhs[side, j, 0:64, :] for j in js],
                [label[j] for j in js],
                [1.0 / found[j] for j in js],
            )
            for j, value in zip(js, values):
                halos[3, side, j] = value
        return carry

    lax.fori_loop(0, 4, halo_sweep, 0)

    for x in range(WIDE):
        for y in range(WIDE):
            own = perm_b[x, y]

            def rim(side, j):
                return jnp.where(inside[side], halo_coarse[0, side, j], 0.0)

            beside = (
                perm_b[x - 1, y] if x > 0 else rim(0, y),
                perm_b[x + 1, y] if x < WIDE - 1 else rim(1, y),
                perm_b[x, y - 1] if y > 0 else rim(2, x),
                perm_b[x, y + 1] if y < WIDE - 1 else rim(3, x),
                jnp.where(lane > 0, pltpu.roll(own, 1, 1), 0.0),
                jnp.where(lane < LANES - 1, pltpu.roll(own, LANES - 1, 1), 0.0),
            )
            there = (
                True if x > 0 else inside[0],
                True if x < WIDE - 1 else inside[1],
                True if y > 0 else inside[2],
                True if y < WIDE - 1 else inside[3],
                lane > 0,
                lane < LANES - 1,
            )
            for d in range(6):
                kn = beside[d]
                w = jnp.where(kn > 0.0, 2.0 * own * kn / (own + kn), 2.0 * own)
                weights[d, x, y] = w
                weights[6 + d, x, y] = w if there[d] is True else jnp.where(there[d], w, 0.0)

    def fine_stack(ref, *lead):
        return lambda x, y: stack_rows(ref[(*lead, x, y)])

    own_products(fine_stack(start_field), op_stack, 64)
    halo_products(fine_stack(halos, 3), op_stack, 64)
    to_owner_middle(0)

    def sweep(residue, iterate, target):
        def one(x, carry):
            for half in range(2):
                ys = (2 * half, 2 * half + 1)
                found = smoothed(
                    [residue(x, y) for y in ys],
                    [label_of(x, y) for y in ys],
                    [perm_inv[x, y] for y in ys],
                )
                for y, value in zip(ys, found):
                    fields[target, x, y] = iterate(x, y) + value
            return carry

        lax.fori_loop(0, WIDE, one, 0)

    sweep(
        lambda x, y: rs[x, y, 0:64, :] - applied(x, y, 64), lambda x, y: start_field[x, y], 0
    )
    send_halo(fields.at[0], halos.at[0], 1)
    own_products(fine_stack(fields, 0), op_stack, 64)

    arrived = to_owner_end(0)
    hot_ids = lax.broadcasted_iota(jnp.int32, (LANES, owners), 0).astype(F32) + 1.0
    for r in range(cap):
        local_hot[:, r * owners : (r + 1) * owners] = jnp.where(
            hot_ids == arrived[8 * r : 8 * r + 1, :], 1.0, 0.0
        ).astype(BF16)
    perm_sum = gather_sum(arrived)[1:2, :]
    coarse_keep[0] = jnp.broadcast_to(1.0 / (1.0 + perm_sum), (8, LANES))

    await_halo(fields.at[0], halos.at[0], 1)
    halo_products(fine_stack(halos, 0), op_stack, 64)

    def second_residue(x, carry):
        rest = []
        for y in range(WIDE):
            value = rs[x, y, 0:64, :] - applied(x, y, 64)
            fine_res[x, y] = value
            rest.append(stack_rows(value))
        found = dot(restrict_cols, jnp.concatenate(rest, axis=1))
        for y in range(WIDE):
            coarse_field[2, x, y] = found[0:8, y * LANES : (y + 1) * LANES]
        return carry

    lax.fori_loop(0, WIDE, second_residue, 0)

    def coarse_step(value):
        product = jnp.dot(
            coarse_ref[...], value, precision=HIGHEST, preferred_element_type=F32
        )
        return coarse_keep[0] * product

    to_owner_start(1, lambda x, y: coarse_field[2, x, y])
    to_owner_middle(1)
    coarse_res = gather_sum(to_owner_end(1))
    first = coarse_step(coarse_res)
    from_owner_start(3, first)
    from_owner_middle(3)
    from_owner_end(3, 0)
    send_halo(coarse_field.at[0], halo_coarse.at[1], 2)
    own_products(fine_stack(coarse_field, 0), coarse_stack, 8)
    await_halo(coarse_field.at[0], halo_coarse.at[1], 2)
    halo_products(fine_stack(halo_coarse, 1), coarse_stack, 8)
    to_owner_start(2, lambda x, y: applied(x, y, 8))
    to_owner_middle(2)
    again = coarse_res - gather_sum(to_owner_end(2))
    second = first + coarse_step(again)
    from_owner_start(4, second)
    from_owner_middle(4)
    from_owner_end(4, 1)
    send_halo(coarse_field.at[1], halo_coarse.at[2], 3)

    def add_prolonged(x, y, value):
        start_field[x, y] = fields[0, x, y] + value

    own_products(fine_stack(coarse_field, 1), prolong_stack, 64, add_prolonged)
    await_halo(coarse_field.at[1], halo_coarse.at[2], 3)
    halo_products(fine_stack(halo_coarse, 2), prolong_stack, 64)
    sweep(lambda x, y: fine_res[x, y] - applied(x, y, 64), lambda x, y: start_field[x, y], 1)
    send_halo(fields.at[1], halos.at[1], 4)

    own_products(fine_stack(fields, 1), op_stack, 64)
    await_halo(fields.at[1], halos.at[1], 4)
    halo_products(fine_stack(halos, 1), op_stack, 64)
    sweep(
        lambda x, y: rs[x, y, 0:64, :] - applied(x, y, 64), lambda x, y: fields[1, x, y], 2
    )
    send_halo(fields.at[2], halos.at[2], 5)
    own_products(fine_stack(fields, 2), op_stack, 64)
    for xy in range(WIDE * WIDE):
        sol_ref[pl.ds(xy, 64, stride=WIDE * WIDE), :] = fields[2, xy // WIDE, xy % WIDE]
    await_halo(fields.at[2], halos.at[2], 5)
    halo_products(fine_stack(halos, 2), op_stack, 64)
    for xy in range(WIDE * WIDE):
        x, y = xy // WIDE, xy % WIDE
        res_ref[pl.ds(xy, 64, stride=WIDE * WIDE), :] = rs[x, y, 0:64, :] - applied(x, y, 64)

    sent = (
        (rs, halo_rhs, 0),
        (fields.at[0], halos.at[0], 1),
        (coarse_field.at[0], halo_coarse.at[1], 2),
        (coarse_field.at[1], halo_coarse.at[2], 3),
        (fields.at[1], halos.at[1], 4),
        (fields.at[2], halos.at[2], 5),
    )
    for source, target, turn in sent:
        for copy in halo_copies(source, target, turn):
            copy.wait_send()
    for turn in range(5):
        release(turn, 0, 0, turn < 3)
        release(turn, 2, 1, turn >= 3)


def local(
    n_slab,
    n_cross,
    cap,
    rhs,
    classes,
    perm,
    vol_block,
    side_blocks,
    couple,
    smoother_blocks,
    restrict_map,
    coarse_block,
    owners,
    agg_local,
):
    vmem = pl.BlockSpec(memory_space=pltpu.VMEM)
    smem = pl.BlockSpec(memory_space=pltpu.SMEM)
    count = n_slab * n_cross
    face = (WIDE, WIDE)
    flat = jax.ShapeDtypeStruct((64 * WIDE * WIDE, LANES), F32)
    scratch = [
        pltpu.VMEM((*face, 72, LANES), F32),
        pltpu.VMEM((4, WIDE, 72, LANES), F32),
        pltpu.VMEM((3, *face, 64, LANES), F32),
        pltpu.VMEM((4, 4, WIDE, 64, LANES), F32),
        pltpu.VMEM((*face, 64, LANES), F32),
        pltpu.VMEM((*face, 64, LANES), F32),
        pltpu.VMEM((*face, 64, LANES), F32),
        pltpu.VMEM((WIDE + 1, WIDE, 64, LANES), F32),
        pltpu.VMEM((WIDE + 1, WIDE, 64, LANES), F32),
        pltpu.VMEM((WIDE, WIDE + 1, 64, LANES), F32),
        pltpu.VMEM((WIDE, WIDE + 1, 64, LANES), F32),
        pltpu.VMEM((14 * 64, 64), F32),
        pltpu.VMEM((13 * 64, 192), BF16),
        pltpu.VMEM((16 * 64, 192), BF16),
        pltpu.VMEM((14 * 64, 32), BF16),
        pltpu.VMEM((14 * 8, 32), BF16),
        pltpu.VMEM((*face, 8, LANES), F32),
        pltpu.VMEM((*face, 8, LANES), F32),
        pltpu.VMEM((12, *face, 8, LANES), F32),
        pltpu.VMEM((2 * count, WIDE * WIDE * LANES), BF16),
        pltpu.VMEM((*face, 8, LANES), F32),
        pltpu.VMEM((2 * cap * 8, WIDE * WIDE * LANES), BF16),
        pltpu.VMEM((LANES, cap * count), BF16),
        pltpu.VMEM((5, 4, cap // 16, count, LANES), F32),
        pltpu.VMEM((1, 8, LANES), F32),
        pltpu.VMEM((3, *face, 8, LANES), F32),
        pltpu.VMEM((3, 4, WIDE, 8, LANES), F32),
        pltpu.SemaphoreType.DMA((6, 4)),
        pltpu.SemaphoreType.DMA((6, 4)),
        pltpu.SemaphoreType.DMA((5, 2)),
        pltpu.SemaphoreType.DMA((5, 2)),
    ]
    flops = 2 * 2048 * (5 * 832 + 5 * 1024) * 192
    solved, residue = pl.pallas_call(
        functools.partial(cycle, n_slab, n_cross, cap),
        out_shape=(flat, flat),
        in_specs=[vmem, vmem, smem] + [vmem] * 8,
        out_specs=(vmem, vmem),
        scratch_shapes=scratch,
        compiler_params=pltpu.CompilerParams(
            collective_id=0, has_side_effects=True, vmem_limit_bytes=56 * 1024 * 1024
        ),
        cost_estimate=pl.CostEstimate(flops=flops, bytes_accessed=4 << 20, transcendentals=0),
    )(
        rhs.reshape(64 * WIDE * WIDE, LANES),
        classes.reshape(WIDE * WIDE, LANES),
        perm,
        vol_block,
        side_blocks.reshape(6 * 64, 64),
        couple.reshape(3 * 64, 64),
        smoother_blocks.reshape(16 * 64, 64),
        restrict_map,
        coarse_block,
        owners.reshape(WIDE * WIDE, LANES),
        agg_local.reshape(WIDE * WIDE, LANES),
    )
    return solved.reshape(rhs.shape), residue.reshape(rhs.shape)


def solution(mesh, cap=32):
    placed = (
        P(None, "slab", "cross", None),
        P("slab", "cross", None),
        P(),
        P(),
        P(),
        P(),
        P(),
        P(),
        P(),
        P("slab", "cross", None, None),
        P("slab", "cross", None),
    )
    return jax.shard_map(
        functools.partial(local, mesh.shape["slab"], mesh.shape["cross"], cap),
        mesh=mesh,
        in_specs=placed,
        out_specs=(P(None, "slab", "cross", None), P(None, "slab", "cross", None)),
        check_vma=False,
    )
```

```python
import functools

import jax
import jax.numpy as jnp
from jax import lax
from jax.experimental import pallas as pl
from jax.experimental.pallas import tpu as pltpu
from jax.sharding import PartitionSpec as P

MESH = pl.DeviceIdType.MESH
F32 = jnp.float32
BF16 = jnp.bfloat16
HIGHEST = lax.Precision.HIGHEST
LANES = 128
WIDE = 4
NT = (((1,), (1,)), ((), ()))


def dot(a, b):
    return jnp.dot(a, b, preferred_element_type=F32)


def dot_nt(a, b):
    return lax.dot_general(a, b, NT, preferred_element_type=F32)


def parts(value):
    high = value.astype(BF16).astype(F32)
    return high, value - high


def stack_rows(value):
    high, low = parts(value)
    pieces = [high, low, high]
    if value.shape[0] == 8:
        pieces.append(jnp.zeros_like(value))
    return jnp.concatenate(pieces, axis=0).astype(BF16)


def stack_columns(value):
    high, low = parts(value)
    pieces = [high, high, low]
    if value.shape[1] == 8:
        pieces.append(jnp.zeros_like(value))
    return jnp.concatenate(pieces, axis=1).astype(BF16)


def cycle(
    n_slab,
    n_cross,
    cap,
    rhs_hbm,
    class_hbm,
    perm_hbm,
    vol_hbm,
    side_hbm,
    couple_hbm,
    smooth_hbm,
    restrict_hbm,
    coarse_hbm,
    owner_hbm,
    local_hbm,
    sol_ref,
    res_ref,
    rhs_ref,
    class_ref,
    perm_ref,
    vol_ref,
    side_ref,
    couple_ref,
    smooth_ref,
    restrict_ref,
    coarse_ref,
    owner_ref,
    local_ref,
    out_ref,
    rs,
    halo_rhs,
    label,
    halo_label,
    fields,
    halos,
    start_field,
    fine_res,
    acc,
    gx0,
    gx1,
    gy0,
    gy1,
    blocks_f32,
    op_stack,
    smooth_stack,
    prolong_stack,
    coarse_stack,
    perm_b,
    perm_inv,
    weights,
    owner_hot,
    rank_b,
    packed,
    local_hot,
    mail,
    coarse_keep,
    coarse_field,
    halo_coarse,
    load_sem,
    halo_send,
    halo_recv,
    mail_send,
    mail_recv,
    all_here,
):
    s, c = lax.axis_index("slab"), lax.axis_index("cross")
    owners = n_slab * n_cross
    s_up, s_down = lax.rem(s + 1, n_slab), lax.rem(s + n_slab - 1, n_slab)
    c_up, c_down = lax.rem(c + 1, n_cross), lax.rem(c + n_cross - 1, n_cross)
    lane = lax.broadcasted_iota(jnp.int32, (8, LANES), 1)

    barrier = pltpu.get_barrier_semaphore()

    def greet_slab(off, carry):
        pl.semaphore_signal(
            barrier, inc=1, device_id=(lax.rem(s + off, n_slab), c), device_id_type=MESH
        )
        return carry

    def greet_cross(off, carry):
        pl.semaphore_signal(
            barrier, inc=1, device_id=(s, lax.rem(c + off, n_cross)), device_id_type=MESH
        )
        return carry

    lax.fori_loop(1, n_slab, greet_slab, 0)
    lax.fori_loop(1, n_cross, greet_cross, 0)

    loads = [
        pltpu.make_async_copy(source, target, load_sem.at[k])
        for k, (source, target) in enumerate(
            (
                (rhs_hbm, rhs_ref),
                (class_hbm, class_ref),
                (perm_hbm, perm_ref),
                (vol_hbm, vol_ref),
                (side_hbm, side_ref),
                (couple_hbm, couple_ref),
                (smooth_hbm, smooth_ref),
                (restrict_hbm, restrict_ref),
                (coarse_hbm, coarse_ref),
                (owner_hbm, owner_ref),
                (local_hbm, local_ref),
            )
        )
    ]
    for copy in loads:
        copy.start()
    loads[0].wait()
    loads[1].wait()

    for xy in range(WIDE * WIDE):
        x, y = xy // WIDE, xy % WIDE
        rs[x, y] = rhs_ref[pl.ds(xy, 64, stride=WIDE * WIDE), :]
        label[x, y] = jnp.broadcast_to(class_ref[xy : xy + 1, :], (8, LANES)).astype(F32)

    pl.semaphore_wait(barrier, n_slab + n_cross - 2)

    sent = []

    def drain():
        for finish in sent:
            finish()

    def halo_copies(source, target, turn):
        plan = (
            (source.at[0], 1, (s_down, c)),
            (source.at[WIDE - 1], 0, (s_up, c)),
            (source.at[:, 0], 3, (s, c_down)),
            (source.at[:, WIDE - 1], 2, (s, c_up)),
        )
        return [
            pltpu.make_async_remote_copy(
                src_ref=face,
                dst_ref=target.at[side],
                send_sem=halo_send.at[turn, side],
                recv_sem=halo_recv.at[turn, side],
                device_id=device,
                device_id_type=MESH,
            )
            for face, side, device in plan
        ]

    def send_halo(source, target, turn):
        for copy in halo_copies(source, target, turn):
            copy.start()
            sent.append(copy.wait_send)

    def await_halo(source, target, turn):
        for copy in halo_copies(source, target, turn):
            copy.wait_recv()

    send_halo(label, halo_label, 6)
    send_halo(rs, halo_rhs, 0)
    for copy in loads[2:]:
        copy.wait()

    def greet_again(off, carry):
        pl.semaphore_signal(
            all_here, inc=1, device_id=(lax.rem(s + off, n_slab), c), device_id_type=MESH
        )
        return carry

    lax.fori_loop(1, n_slab, greet_again, 0)

    blocks_f32[0:64, :] = vol_ref[...]
    blocks_f32[64:448, :] = side_ref[...]
    for m in range(3):
        plus = couple_ref[m * 64 : (m + 1) * 64, :]
        blocks_f32[448 + 128 * m : 512 + 128 * m, :] = plus.T
        blocks_f32[512 + 128 * m : 576 + 128 * m, :] = plus
    blocks_f32[832:896, :] = jnp.where(
        lax.broadcasted_iota(jnp.int32, (64, 64), 0) == lax.broadcasted_iota(jnp.int32, (64, 64), 1),
        1.0,
        0.0,
    )
    for m in range(13):
        rows = slice(64 * m, 64 * m + 64)
        op_stack[rows, :] = stack_columns(blocks_f32[rows, :])
    for m in range(16):
        rows = slice(64 * m, 64 * m + 64)
        smooth_stack[rows, :] = stack_columns(smooth_ref[rows, :])
    restrict = restrict_ref[...]
    short = lax.dot_general(
        blocks_f32[...], restrict, NT, precision=HIGHEST, preferred_element_type=F32
    )
    prolong_stack[...] = stack_columns(short)
    tiny = [
        jnp.dot(restrict, short[64 * m : 64 * m + 64], precision=HIGHEST, preferred_element_type=F32)
        for m in range(13)
    ]
    coarse_stack[...] = stack_columns(jnp.concatenate(tiny + [jnp.zeros((8, 8), F32)], axis=0))
    restrict_cols = stack_columns(jnp.concatenate([restrict, jnp.zeros_like(restrict)], axis=0))

    hot_rows = lax.broadcasted_iota(jnp.int32, (owners, LANES), 0)
    before = jnp.concatenate(
        [
            jnp.where(
                lax.broadcasted_iota(jnp.int32, (LANES, LANES), 0)
                < lax.broadcasted_iota(jnp.int32, (LANES, LANES), 1),
                1.0,
                0.0,
            ),
            jnp.ones((LANES, LANES), F32),
        ],
        axis=1,
    ).astype(BF16)
    seen = jnp.zeros((owners, LANES), F32)
    for xy in range(WIDE * WIDE):
        x, y = xy // WIDE, xy % WIDE
        hot = jnp.where(hot_rows == owner_ref[xy : xy + 1, :], 1.0, 0.0)
        hot_low = hot.astype(BF16)
        owner_hot[0:owners, xy * LANES : (xy + 1) * LANES] = hot_low
        owner_hot[owners : 2 * owners, xy * LANES : (xy + 1) * LANES] = hot_low
        counted = dot(hot_low, before)
        rank = jnp.sum(hot * (counted[:, 0:LANES] + seen), axis=0, keepdims=True)
        seen = seen + counted[:, LANES : 2 * LANES]
        rank_b[x, y] = jnp.broadcast_to(rank, (8, LANES))

    def perm_of(kind):
        value = jnp.zeros_like(kind)
        for k in range(16):
            value = jnp.where(kind == float(k), perm_ref[k], value)
        return value

    def own_perm(x, carry):
        for y in range(WIDE):
            value = perm_of(label[x, y])
            perm_b[x, y] = value
            perm_inv[x, y] = 1.0 / value
        return carry

    lax.fori_loop(0, WIDE, own_perm, 0)

    side_y = WIDE
    side_x = n_slab // side_y
    me = s * n_cross + c
    s_x, s_y = s // side_y, lax.rem(s, side_y)

    def hops(step):
        return min(step[0], side_x - step[0]) + min(step[1], side_y - step[1])

    far_first = sorted(
        ((i, j) for i in range(side_x) for j in range(side_y)), key=lambda step: -hops(step)
    )

    def post(turn):
        for step in far_first:
            to_slab = lax.rem(s_x + step[0], side_x) * side_y + lax.rem(s_y + step[1], side_y)

            def one(off, carry):
                to_cross = lax.rem(c + off, n_cross)
                pltpu.make_async_remote_copy(
                    src_ref=mail.at[turn, 0, to_slab * n_cross + to_cross],
                    dst_ref=mail.at[turn, 1, me],
                    send_sem=mail_send.at[turn],
                    recv_sem=mail_recv.at[turn],
                    device_id=(to_slab, to_cross),
                    device_id_type=MESH,
                ).start()
                return carry

            lax.fori_loop(0 if hops(step) else 1, n_cross, one, 0)
        sent.append(functools.partial(release, turn))
        mail[turn, 1, me] = mail[turn, 0, me]

    def collect(turn):
        part = mail.at[turn, 1, pl.ds(0, owners - 1)]
        pltpu.make_async_copy(part, part, mail_recv.at[turn]).wait()

    def release(turn):
        part = mail.at[turn, 0, pl.ds(0, owners - 1)]
        pltpu.make_async_copy(part, part, mail_send.at[turn]).wait()

    def write_mail(turn, value):
        mail[turn, 0] = value.reshape(owners, cap // 16, LANES)

    def read_mail(turn):
        return mail[turn, 1].reshape(owners, cap * 8).T

    def pack(load):
        def one(x, carry):
            for y in range(WIDE):
                rank = rank_b[x, y]
                keep = [rank == float(r) for r in range(cap)]
                columns = pl.ds(pl.multiple_of((x * WIDE + y) * LANES, LANES), LANES)
                for i, piece in enumerate(parts(load(x, y))):
                    spread = jnp.concatenate([jnp.where(k, piece, 0.0) for k in keep], axis=0)
                    packed[i * cap * 8 : (i + 1) * cap * 8, columns] = spread.astype(BF16)
            return carry

        lax.fori_loop(0, WIDE, one, 0)

    def to_owner_start(turn, load):
        pack(load)
        slots = dot_nt(owner_hot[0:owners, :], packed[...])
        write_mail(turn, slots[:, 0 : cap * 8] + slots[:, cap * 8 : 2 * cap * 8])
        post(turn)

    def to_owner_end(turn):
        collect(turn)
        return read_mail(turn)

    def gather_sum(arrived):
        flat = jnp.concatenate([arrived[8 * r : 8 * r + 8] for r in range(cap)], axis=1)
        high, low = parts(flat)
        both = dot_nt(jnp.concatenate([high, low], axis=0).astype(BF16), local_hot[...])
        return both[0:8] + both[8:16]

    def from_owner_start(turn, value):
        high, low = parts(value)
        both = dot(jnp.concatenate([high, low], axis=0).astype(BF16), local_hot[...])
        flat = both[0:8] + both[8:16]
        out = jnp.concatenate([flat[:, owners * r : owners * (r + 1)] for r in range(cap)], axis=0)
        write_mail(turn, out.T)
        post(turn)

    def from_owner_end(turn, target):
        collect(turn)
        high, low = parts(read_mail(turn))
        spread = jnp.concatenate([high, low], axis=1).astype(BF16)
        for pair in range(WIDE * WIDE // 2):
            both = dot(spread, owner_hot[:, pair * 2 * LANES : (pair + 1) * 2 * LANES])
            for i in range(2):
                x, y = (2 * pair + i) // WIDE, (2 * pair + i) % WIDE
                rank = rank_b[x, y]
                value = jnp.zeros((8, LANES), F32)
                for r in range(cap):
                    value = jnp.where(
                        rank == float(r),
                        both[8 * r : 8 * r + 8, i * LANES : (i + 1) * LANES],
                        value,
                    )
                coarse_field[target, x, y] = value

    def own_products(load, stack, rows, extra=None):
        def one(x, carry):
            for half in range(2):
                ys = (2 * half, 2 * half + 1)
                product = dot(stack[...], jnp.concatenate([load(x, y) for y in ys], axis=1))
                for i, y in enumerate(ys):

                    def block(b):
                        return product[b * rows : (b + 1) * rows, i * LANES : (i + 1) * LANES]

                    def scaled(weight, value):
                        return weight[None] * value.reshape(rows // 8, 8, LANES)

                    total = scaled(perm_b[x, y], block(0))
                    for d in range(6):
                        total = total + scaled(weights[d, x, y], block(1 + d))
                    total = total - scaled(weights[10, x, y], pltpu.roll(block(11), 1, 1))
                    total = total - scaled(weights[11, x, y], pltpu.roll(block(12), LANES - 1, 1))
                    acc[x, y, 0:rows, :] = total.reshape(rows, LANES)
                    gx0[x + 1, y, 0:rows, :] = block(7)
                    gx1[x, y, 0:rows, :] = block(8)
                    gy0[x, y + 1, 0:rows, :] = block(9)
                    gy1[x, y, 0:rows, :] = block(10)
                    if extra is not None:
                        extra(x, y, block(13))
            return carry

        lax.fori_loop(0, WIDE, one, 0)

    def halo_products(load, stack, rows):
        for side in range(4):
            data = jnp.concatenate([load(side, j) for j in range(WIDE)], axis=1)
            if rows == 64:
                product = dot(stack[(7 + side) * rows : (8 + side) * rows, :], data)
            else:
                product = dot(stack[...], data)[(7 + side) * rows : (8 + side) * rows]
            for j in range(WIDE):
                value = product[:, j * LANES : (j + 1) * LANES]
                if side == 0:
                    gx0[0, j, 0:rows, :] = value
                elif side == 1:
                    gx1[WIDE, j, 0:rows, :] = value
                elif side == 2:
                    gy0[j, 0, 0:rows, :] = value
                else:
                    gy1[j, WIDE, 0:rows, :] = value

    def applied(x, y, rows):
        def scaled(weight, value):
            return weight[None] * value.reshape(rows // 8, 8, LANES)

        total = acc[x, y, 0:rows, :].reshape(rows // 8, 8, LANES)
        total = total - scaled(weights[6, x, y], gx0[x, y, 0:rows, :])
        total = total - scaled(weights[7, x, y], gx1[x + 1, y, 0:rows, :])
        total = total - scaled(weights[8, x, y], gy0[x, y, 0:rows, :])
        total = total - scaled(weights[9, x, y], gy1[x, y + 1, 0:rows, :])
        return total.reshape(rows, LANES)

    def smoothed(values, labels, inverses):
        product = dot(smooth_stack[...], jnp.concatenate([stack_rows(v) for v in values], axis=1))
        results = []
        for i, (label, inverse) in enumerate(zip(labels, inverses)):
            columns = slice(i * LANES, (i + 1) * LANES)
            value = product[0:64, columns].reshape(8, 8, LANES)
            for k in range(1, 16):
                block = product[64 * k : 64 * k + 64, columns].reshape(8, 8, LANES)
                value = jnp.where((label == float(k))[None], block, value)
            results.append((value * inverse[None]).reshape(64, LANES))
        return results

    def label_of(x, y):
        return label[x, y]

    def first_sweep(x, carry):
        for half in range(2):
            ys = (2 * half, 2 * half + 1)
            found = smoothed(
                [rs[x, y] for y in ys],
                [label_of(x, y) for y in ys],
                [perm_inv[x, y] for y in ys],
            )
            for y, value in zip(ys, found):
                start_field[x, y] = value
        return carry

    lax.fori_loop(0, WIDE, first_sweep, 0)

    def keys(x, y):
        row = lax.broadcasted_iota(jnp.int32, (8, LANES), 0)
        label = jnp.broadcast_to(local_ref[pl.ds(x * WIDE + y, 1), :], (8, LANES)).astype(F32) + 1.0
        return jnp.where(row == 0, label, jnp.where(row == 1, perm_b[x, y], 0.0))

    pl.semaphore_wait(all_here, n_slab - 1)
    to_owner_start(0, keys)

    await_halo(label, halo_label, 6)
    inside = (s > 0, s < n_slab - 1, c > 0, c < n_cross - 1)
    for side in range(4):
        for j in range(WIDE):
            halo_coarse[0, side, j] = perm_of(halo_label[side, j])

    for x in range(WIDE):
        for y in range(WIDE):
            own = perm_b[x, y]

            def rim(side, j):
                return jnp.where(inside[side], halo_coarse[0, side, j], 0.0)

            beside = (
                perm_b[x - 1, y] if x > 0 else rim(0, y),
                perm_b[x + 1, y] if x < WIDE - 1 else rim(1, y),
                perm_b[x, y - 1] if y > 0 else rim(2, x),
                perm_b[x, y + 1] if y < WIDE - 1 else rim(3, x),
                jnp.where(lane > 0, pltpu.roll(own, 1, 1), 0.0),
                jnp.where(lane < LANES - 1, pltpu.roll(own, LANES - 1, 1), 0.0),
            )
            there = (
                True if x > 0 else inside[0],
                True if x < WIDE - 1 else inside[1],
                True if y > 0 else inside[2],
                True if y < WIDE - 1 else inside[3],
                lane > 0,
                lane < LANES - 1,
            )
            for d in range(6):
                kn = beside[d]
                w = jnp.where(kn > 0.0, 2.0 * own * kn / (own + kn), 2.0 * own)
                weights[d, x, y] = w
                weights[6 + d, x, y] = w if there[d] is True else jnp.where(there[d], w, 0.0)

    def fine_stack(ref, *lead):
        return lambda x, y: stack_rows(ref[(*lead, x, y)])

    own_products(fine_stack(start_field), op_stack, 64)

    await_halo(rs, halo_rhs, 0)

    def halo_sweep(side, carry):
        for half in range(2):
            js = (2 * half, 2 * half + 1)
            values = smoothed(
                [halo_rhs[side, j] for j in js],
                [halo_label[side, j] for j in js],
                [1.0 / halo_coarse[0, side, j] for j in js],
            )
            for j, value in zip(js, values):
                halos[3, side, j] = value
        return carry

    lax.fori_loop(0, 4, halo_sweep, 0)
    halo_products(fine_stack(halos, 3), op_stack, 64)

    def sweep(residue, iterate, target, turn):
        def one(step, carry):
            x = lax.rem(step * 3, WIDE)
            for half in range(2):
                ys = (2 * half, 2 * half + 1)
                found = smoothed(
                    [residue(x, y) for y in ys],
                    [label_of(x, y) for y in ys],
                    [perm_inv[x, y] for y in ys],
                )
                for y, value in zip(ys, found):
                    fields[target, x, y] = iterate(x, y) + value

            @pl.when(step == 0)
            def _():
                halo_copies(fields.at[target], halos.at[target], turn)[0].start()

            @pl.when(step == 1)
            def _():
                halo_copies(fields.at[target], halos.at[target], turn)[1].start()

            return carry

        lax.fori_loop(0, WIDE, one, 0)
        copies = halo_copies(fields.at[target], halos.at[target], turn)
        copies[2].start()
        copies[3].start()
        sent.extend(copy.wait_send for copy in copies)

    sweep(
        lambda x, y: rs[x, y] - applied(x, y, 64), lambda x, y: start_field[x, y], 0, 1
    )
    own_products(fine_stack(fields, 0), op_stack, 64)

    arrived = to_owner_end(0)
    hot_ids = lax.broadcasted_iota(jnp.int32, (LANES, owners), 0).astype(F32) + 1.0
    for r in range(cap):
        local_hot[:, r * owners : (r + 1) * owners] = jnp.where(
            hot_ids == arrived[8 * r : 8 * r + 1, :], 1.0, 0.0
        ).astype(BF16)
    perm_sum = gather_sum(arrived)[1:2, :]
    coarse_keep[0] = jnp.broadcast_to(1.0 / (1.0 + perm_sum), (8, LANES))

    await_halo(fields.at[0], halos.at[0], 1)
    halo_products(fine_stack(halos, 0), op_stack, 64)

    def second_residue(x, carry):
        rest = []
        for y in range(WIDE):
            value = rs[x, y] - applied(x, y, 64)
            fine_res[x, y] = value
            rest.append(stack_rows(value))
        found = dot(restrict_cols, jnp.concatenate(rest, axis=1))
        for y in range(WIDE):
            coarse_field[2, x, y] = found[0:8, y * LANES : (y + 1) * LANES]
        return carry

    lax.fori_loop(0, WIDE, second_residue, 0)

    def coarse_step(value):
        product = jnp.dot(
            coarse_ref[...], value, precision=HIGHEST, preferred_element_type=F32
        )
        return coarse_keep[0] * product

    to_owner_start(1, lambda x, y: coarse_field[2, x, y])
    coarse_res = gather_sum(to_owner_end(1))
    first = coarse_step(coarse_res)
    from_owner_start(3, first)
    from_owner_end(3, 0)
    send_halo(coarse_field.at[0], halo_coarse.at[1], 2)
    own_products(fine_stack(coarse_field, 0), coarse_stack, 8)
    await_halo(coarse_field.at[0], halo_coarse.at[1], 2)
    halo_products(fine_stack(halo_coarse, 1), coarse_stack, 8)
    to_owner_start(2, lambda x, y: applied(x, y, 8))
    again = coarse_res - gather_sum(to_owner_end(2))
    second = first + coarse_step(again)
    from_owner_start(4, second)
    from_owner_end(4, 1)
    send_halo(coarse_field.at[1], halo_coarse.at[2], 3)

    def add_prolonged(x, y, value):
        start_field[x, y] = fields[0, x, y] + value

    own_products(fine_stack(coarse_field, 1), prolong_stack, 64, add_prolonged)
    await_halo(coarse_field.at[1], halo_coarse.at[2], 3)
    halo_products(fine_stack(halo_coarse, 2), prolong_stack, 64)
    sweep(lambda x, y: fine_res[x, y] - applied(x, y, 64), lambda x, y: start_field[x, y], 1, 4)

    own_products(fine_stack(fields, 1), op_stack, 64)
    await_halo(fields.at[1], halos.at[1], 4)
    halo_products(fine_stack(halos, 1), op_stack, 64)
    sweep(
        lambda x, y: rs[x, y] - applied(x, y, 64), lambda x, y: fields[1, x, y], 2, 5
    )
    own_products(fine_stack(fields, 2), op_stack, 64)
    for xy in range(WIDE * WIDE):
        rhs_ref[pl.ds(xy, 64, stride=WIDE * WIDE), :] = fields[2, xy // WIDE, xy % WIDE]
    store = pltpu.make_async_copy(rhs_ref, sol_ref, load_sem.at[0])
    store.start()
    await_halo(fields.at[2], halos.at[2], 5)
    halo_products(fine_stack(halos, 2), op_stack, 64)
    for xy in range(WIDE * WIDE):
        x, y = xy // WIDE, xy % WIDE
        out_ref[pl.ds(xy, 64, stride=WIDE * WIDE), :] = rs[x, y] - applied(x, y, 64)

    last = pltpu.make_async_copy(out_ref, res_ref, load_sem.at[1])
    last.start()
    drain()
    store.wait()
    last.wait()


def hand_over(sol_in, res_in, sol_out, res_out, sem):
    copies = [
        pltpu.make_async_copy(sol_in, sol_out, sem.at[0]),
        pltpu.make_async_copy(res_in, res_out, sem.at[1]),
    ]
    for copy in copies:
        copy.start()
    for copy in copies:
        copy.wait()


def local(
    n_slab,
    n_cross,
    cap,
    rhs,
    classes,
    perm,
    vol_block,
    side_blocks,
    couple,
    smoother_blocks,
    restrict_map,
    coarse_block,
    owners,
    agg_local,
):
    anywhere = pl.BlockSpec(memory_space=pl.ANY)
    count = n_slab * n_cross
    face = (WIDE, WIDE)
    flat = jax.ShapeDtypeStruct((64 * WIDE * WIDE, LANES), F32)
    scratch = [
        pltpu.VMEM((64 * WIDE * WIDE, LANES), F32),
        pltpu.VMEM((WIDE * WIDE, LANES), jnp.int32),
        pltpu.SMEM((16,), F32),
        pltpu.VMEM((64, 64), F32),
        pltpu.VMEM((6 * 64, 64), F32),
        pltpu.VMEM((3 * 64, 64), F32),
        pltpu.VMEM((16 * 64, 64), F32),
        pltpu.VMEM((8, 64), F32),
        pltpu.VMEM((8, 8), F32),
        pltpu.VMEM((WIDE * WIDE, LANES), jnp.int32),
        pltpu.VMEM((WIDE * WIDE, LANES), jnp.int32),
        pltpu.VMEM((64 * WIDE * WIDE, LANES), F32),
        pltpu.VMEM((*face, 64, LANES), F32),
        pltpu.VMEM((4, WIDE, 64, LANES), F32),
        pltpu.VMEM((*face, 8, LANES), F32),
        pltpu.VMEM((4, WIDE, 8, LANES), F32),
        pltpu.VMEM((3, *face, 64, LANES), F32),
        pltpu.VMEM((4, 4, WIDE, 64, LANES), F32),
        pltpu.VMEM((*face, 64, LANES), F32),
        pltpu.VMEM((*face, 64, LANES), F32),
        pltpu.VMEM((*face, 64, LANES), F32),
        pltpu.VMEM((WIDE + 1, WIDE, 64, LANES), F32),
        pltpu.VMEM((WIDE + 1, WIDE, 64, LANES), F32),
        pltpu.VMEM((WIDE, WIDE + 1, 64, LANES), F32),
        pltpu.VMEM((WIDE, WIDE + 1, 64, LANES), F32),
        pltpu.VMEM((14 * 64, 64), F32),
        pltpu.VMEM((13 * 64, 192), BF16),
        pltpu.VMEM((16 * 64, 192), BF16),
        pltpu.VMEM((14 * 64, 32), BF16),
        pltpu.VMEM((14 * 8, 32), BF16),
        pltpu.VMEM((*face, 8, LANES), F32),
        pltpu.VMEM((*face, 8, LANES), F32),
        pltpu.VMEM((12, *face, 8, LANES), F32),
        pltpu.VMEM((2 * count, WIDE * WIDE * LANES), BF16),
        pltpu.VMEM((*face, 8, LANES), F32),
        pltpu.VMEM((2 * cap * 8, WIDE * WIDE * LANES), BF16),
        pltpu.VMEM((LANES, cap * count), BF16),
        pltpu.VMEM((5, 2, count, cap // 16, LANES), F32),
        pltpu.VMEM((1, 8, LANES), F32),
        pltpu.VMEM((3, *face, 8, LANES), F32),
        pltpu.VMEM((3, 4, WIDE, 8, LANES), F32),
        pltpu.SemaphoreType.DMA((11,)),
        pltpu.SemaphoreType.DMA((7, 4)),
        pltpu.SemaphoreType.DMA((7, 4)),
        pltpu.SemaphoreType.DMA((5,)),
        pltpu.SemaphoreType.DMA((5,)),
        pltpu.SemaphoreType.REGULAR,
    ]
    flops = 2 * 2048 * (5 * 832 + 5 * 1024) * 192
    solved, residue = pl.pallas_call(
        functools.partial(cycle, n_slab, n_cross, cap),
        out_shape=(flat, flat),
        in_specs=[pl.BlockSpec(memory_space=pltpu.HBM)] * 11,
        out_specs=(anywhere, anywhere),
        scratch_shapes=scratch,
        compiler_params=pltpu.CompilerParams(
            collective_id=0, has_side_effects=True, vmem_limit_bytes=62 * 1024 * 1024
        ),
        cost_estimate=pl.CostEstimate(flops=flops, bytes_accessed=4 << 20, transcendentals=0),
    )(
        rhs.reshape(64 * WIDE * WIDE, LANES),
        classes.reshape(WIDE * WIDE, LANES),
        perm,
        vol_block,
        side_blocks.reshape(6 * 64, 64),
        couple.reshape(3 * 64, 64),
        smoother_blocks.reshape(16 * 64, 64),
        restrict_map,
        coarse_block,
        owners.reshape(WIDE * WIDE, LANES),
        agg_local.reshape(WIDE * WIDE, LANES),
    )
    solved, residue = pl.pallas_call(
        hand_over,
        out_shape=(flat, flat),
        in_specs=[anywhere] * 2,
        out_specs=(anywhere, anywhere),
        scratch_shapes=[pltpu.SemaphoreType.DMA((2,))],
        compiler_params=pltpu.CompilerParams(vmem_limit_bytes=62 * 1024 * 1024),
    )(solved, residue)
    return solved.reshape(rhs.shape), residue.reshape(rhs.shape)


def solution(mesh, cap=32):
    placed = (
        P(None, "slab", "cross", None),
        P("slab", "cross", None),
        P(),
        P(),
        P(),
        P(),
        P(),
        P(),
        P(),
        P("slab", "cross", None, None),
        P("slab", "cross", None),
    )
    return jax.shard_map(
        functools.partial(local, mesh.shape["slab"], mesh.shape["cross"], cap),
        mesh=mesh,
        in_specs=placed,
        out_specs=(P(None, "slab", "cross", None), P(None, "slab", "cross", None)),
        check_vma=False,
    )
```

```python
import functools

import jax
import jax.numpy as jnp
from jax import lax
from jax.experimental import pallas as pl
from jax.experimental.pallas import tpu as pltpu
from jax.sharding import PartitionSpec as P

MESH = pl.DeviceIdType.MESH
F32 = jnp.float32
BF16 = jnp.bfloat16
HIGHEST = lax.Precision.HIGHEST
LANES = 128
WIDE = 4
NT = (((1,), (1,)), ((), ()))


def dot(a, b):
    return jnp.dot(a, b, preferred_element_type=F32)


def dot_nt(a, b):
    return lax.dot_general(a, b, NT, preferred_element_type=F32)


def parts(value):
    high = value.astype(BF16).astype(F32)
    return high, value - high


def stack_rows(value):
    high, low = parts(value)
    pieces = [high, low, high]
    if value.shape[0] == 8:
        pieces.append(jnp.zeros_like(value))
    return jnp.concatenate(pieces, axis=0).astype(BF16)


def stack_columns(value):
    high, low = parts(value)
    pieces = [high, high, low]
    if value.shape[1] == 8:
        pieces.append(jnp.zeros_like(value))
    return jnp.concatenate(pieces, axis=1).astype(BF16)


def cycle(
    n_slab,
    n_cross,
    cap,
    rhs_hbm,
    class_hbm,
    perm_hbm,
    vol_hbm,
    side_hbm,
    couple_hbm,
    smooth_hbm,
    restrict_hbm,
    coarse_hbm,
    owner_hbm,
    local_hbm,
    sol_ref,
    res_ref,
    rhs_ref,
    class_ref,
    perm_ref,
    vol_ref,
    side_ref,
    couple_ref,
    smooth_ref,
    restrict_ref,
    coarse_ref,
    owner_ref,
    local_ref,
    rs,
    halo_rhs,
    label,
    halo_label,
    fields,
    halos,
    start_field,
    fine_res,
    acc,
    gx0,
    gx1,
    gy0,
    gy1,
    blocks_f32,
    op_stack,
    smooth_stack,
    prolong_stack,
    coarse_stack,
    perm_b,
    perm_inv,
    weights,
    owner_hot,
    rank_b,
    packed,
    local_hot,
    mail,
    coarse_keep,
    coarse_field,
    halo_coarse,
    load_sem,
    halo_send,
    halo_recv,
    mail_send,
    mail_recv,
    all_here,
):
    s, c = lax.axis_index("slab"), lax.axis_index("cross")
    owners = n_slab * n_cross
    s_up, s_down = lax.rem(s + 1, n_slab), lax.rem(s + n_slab - 1, n_slab)
    c_up, c_down = lax.rem(c + 1, n_cross), lax.rem(c + n_cross - 1, n_cross)
    lane = lax.broadcasted_iota(jnp.int32, (8, LANES), 1)

    barrier = pltpu.get_barrier_semaphore()

    def greet_slab(off, carry):
        pl.semaphore_signal(
            barrier, inc=1, device_id=(lax.rem(s + off, n_slab), c), device_id_type=MESH
        )
        return carry

    def greet_cross(off, carry):
        pl.semaphore_signal(
            barrier, inc=1, device_id=(s, lax.rem(c + off, n_cross)), device_id_type=MESH
        )
        return carry

    lax.fori_loop(1, n_slab, greet_slab, 0)
    lax.fori_loop(1, n_cross, greet_cross, 0)

    loads = [
        pltpu.make_async_copy(source, target, load_sem.at[k])
        for k, (source, target) in enumerate(
            (
                (rhs_hbm, rhs_ref),
                (class_hbm, class_ref),
                (perm_hbm, perm_ref),
                (vol_hbm, vol_ref),
                (side_hbm, side_ref),
                (couple_hbm, couple_ref),
                (smooth_hbm, smooth_ref),
                (restrict_hbm, restrict_ref),
                (coarse_hbm, coarse_ref),
                (owner_hbm, owner_ref),
                (local_hbm, local_ref),
            )
        )
    ]
    for copy in loads:
        copy.start()
    loads[0].wait()
    loads[1].wait()

    for xy in range(WIDE * WIDE):
        x, y = xy // WIDE, xy % WIDE
        rs[x, y] = rhs_ref[pl.ds(xy, 64, stride=WIDE * WIDE), :]
        label[x, y] = jnp.broadcast_to(class_ref[xy : xy + 1, :], (8, LANES)).astype(F32)

    pl.semaphore_wait(barrier, n_slab + n_cross - 2)

    sent = []

    def drain():
        for finish in sent:
            finish()

    def halo_copies(source, target, turn):
        plan = (
            (source.at[0], 1, (s_down, c)),
            (source.at[WIDE - 1], 0, (s_up, c)),
            (source.at[:, 0], 3, (s, c_down)),
            (source.at[:, WIDE - 1], 2, (s, c_up)),
        )
        return [
            pltpu.make_async_remote_copy(
                src_ref=face,
                dst_ref=target.at[side],
                send_sem=halo_send.at[turn, side],
                recv_sem=halo_recv.at[turn, side],
                device_id=device,
                device_id_type=MESH,
            )
            for face, side, device in plan
        ]

    def send_halo(source, target, turn):
        for copy in halo_copies(source, target, turn):
            copy.start()
            sent.append(copy.wait_send)

    def await_halo(source, target, turn):
        for copy in halo_copies(source, target, turn):
            copy.wait_recv()

    send_halo(label, halo_label, 6)
    send_halo(rs, halo_rhs, 0)
    for copy in loads[2:]:
        copy.wait()

    def greet_again(off, carry):
        pl.semaphore_signal(
            all_here, inc=1, device_id=(lax.rem(s + off, n_slab), c), device_id_type=MESH
        )
        return carry

    lax.fori_loop(1, n_slab, greet_again, 0)

    blocks_f32[0:64, :] = vol_ref[...]
    blocks_f32[64:448, :] = side_ref[...]
    for m in range(3):
        plus = couple_ref[m * 64 : (m + 1) * 64, :]
        blocks_f32[448 + 128 * m : 512 + 128 * m, :] = plus.T
        blocks_f32[512 + 128 * m : 576 + 128 * m, :] = plus
    blocks_f32[832:896, :] = jnp.where(
        lax.broadcasted_iota(jnp.int32, (64, 64), 0) == lax.broadcasted_iota(jnp.int32, (64, 64), 1),
        1.0,
        0.0,
    )
    for m in range(13):
        rows = slice(64 * m, 64 * m + 64)
        op_stack[rows, :] = stack_columns(blocks_f32[rows, :])
    for m in range(16):
        rows = slice(64 * m, 64 * m + 64)
        smooth_stack[rows, :] = stack_columns(smooth_ref[rows, :])
    restrict = restrict_ref[...]
    short = lax.dot_general(
        blocks_f32[...], restrict, NT, precision=HIGHEST, preferred_element_type=F32
    )
    prolong_stack[...] = stack_columns(short)
    tiny = [
        jnp.dot(restrict, short[64 * m : 64 * m + 64], precision=HIGHEST, preferred_element_type=F32)
        for m in range(13)
    ]
    coarse_stack[...] = stack_columns(jnp.concatenate(tiny + [jnp.zeros((8, 8), F32)], axis=0))
    restrict_cols = stack_columns(jnp.concatenate([restrict, jnp.zeros_like(restrict)], axis=0))

    hot_rows = lax.broadcasted_iota(jnp.int32, (owners, LANES), 0)
    before = jnp.concatenate(
        [
            jnp.where(
                lax.broadcasted_iota(jnp.int32, (LANES, LANES), 0)
                < lax.broadcasted_iota(jnp.int32, (LANES, LANES), 1),
                1.0,
                0.0,
            ),
            jnp.ones((LANES, LANES), F32),
        ],
        axis=1,
    ).astype(BF16)
    seen = jnp.zeros((owners, LANES), F32)
    for xy in range(WIDE * WIDE):
        x, y = xy // WIDE, xy % WIDE
        hot = jnp.where(hot_rows == owner_ref[xy : xy + 1, :], 1.0, 0.0)
        hot_low = hot.astype(BF16)
        owner_hot[0:owners, xy * LANES : (xy + 1) * LANES] = hot_low
        owner_hot[owners : 2 * owners, xy * LANES : (xy + 1) * LANES] = hot_low
        counted = dot(hot_low, before)
        rank = jnp.sum(hot * (counted[:, 0:LANES] + seen), axis=0, keepdims=True)
        seen = seen + counted[:, LANES : 2 * LANES]
        rank_b[x, y] = jnp.broadcast_to(rank, (8, LANES))

    def perm_of(kind):
        value = jnp.zeros_like(kind)
        for k in range(16):
            value = jnp.where(kind == float(k), perm_ref[k], value)
        return value

    def own_perm(x, carry):
        for y in range(WIDE):
            value = perm_of(label[x, y])
            perm_b[x, y] = value
            perm_inv[x, y] = 1.0 / value
        return carry

    lax.fori_loop(0, WIDE, own_perm, 0)

    side_y = WIDE
    side_x = n_slab // side_y
    me = s * n_cross + c
    s_x, s_y = s // side_y, lax.rem(s, side_y)

    def hops(step):
        return min(step[0], side_x - step[0]) + min(step[1], side_y - step[1])

    far_first = sorted(
        ((i, j) for i in range(side_x) for j in range(side_y)), key=lambda step: -hops(step)
    )

    def post(turn):
        for step in far_first:
            to_slab = lax.rem(s_x + step[0], side_x) * side_y + lax.rem(s_y + step[1], side_y)

            def one(off, carry):
                to_cross = lax.rem(c + off, n_cross)
                pltpu.make_async_remote_copy(
                    src_ref=mail.at[turn, 0, to_slab * n_cross + to_cross],
                    dst_ref=mail.at[turn, 1, me],
                    send_sem=mail_send.at[turn],
                    recv_sem=mail_recv.at[turn],
                    device_id=(to_slab, to_cross),
                    device_id_type=MESH,
                ).start()
                return carry

            lax.fori_loop(0 if hops(step) else 1, n_cross, one, 0)
        sent.append(functools.partial(release, turn))
        mail[turn, 1, me] = mail[turn, 0, me]

    def collect(turn):
        part = mail.at[turn, 1, pl.ds(0, owners - 1)]
        pltpu.make_async_copy(part, part, mail_recv.at[turn]).wait()

    def release(turn):
        part = mail.at[turn, 0, pl.ds(0, owners - 1)]
        pltpu.make_async_copy(part, part, mail_send.at[turn]).wait()

    def write_mail(turn, value):
        mail[turn, 0] = value.reshape(owners, cap // 16, LANES)

    def read_mail(turn):
        return mail[turn, 1].reshape(owners, cap * 8).T

    def pack(load):
        def one(x, carry):
            for y in range(WIDE):
                rank = rank_b[x, y]
                keep = [rank == float(r) for r in range(cap)]
                columns = pl.ds(pl.multiple_of((x * WIDE + y) * LANES, LANES), LANES)
                for i, piece in enumerate(parts(load(x, y))):
                    spread = jnp.concatenate([jnp.where(k, piece, 0.0) for k in keep], axis=0)
                    packed[i * cap * 8 : (i + 1) * cap * 8, columns] = spread.astype(BF16)
            return carry

        lax.fori_loop(0, WIDE, one, 0)

    def to_owner_start(turn, load):
        pack(load)
        slots = dot_nt(owner_hot[0:owners, :], packed[...])
        write_mail(turn, slots[:, 0 : cap * 8] + slots[:, cap * 8 : 2 * cap * 8])
        post(turn)

    def to_owner_end(turn):
        collect(turn)
        return read_mail(turn)

    def gather_sum(arrived):
        flat = jnp.concatenate([arrived[8 * r : 8 * r + 8] for r in range(cap)], axis=1)
        high, low = parts(flat)
        both = dot_nt(jnp.concatenate([high, low], axis=0).astype(BF16), local_hot[...])
        return both[0:8] + both[8:16]

    def from_owner_start(turn, value):
        high, low = parts(value)
        both = dot(jnp.concatenate([high, low], axis=0).astype(BF16), local_hot[...])
        flat = both[0:8] + both[8:16]
        out = jnp.concatenate([flat[:, owners * r : owners * (r + 1)] for r in range(cap)], axis=0)
        write_mail(turn, out.T)
        post(turn)

    def from_owner_end(turn, target):
        collect(turn)
        high, low = parts(read_mail(turn))
        spread = jnp.concatenate([high, low], axis=1).astype(BF16)
        for pair in range(WIDE * WIDE // 2):
            both = dot(spread, owner_hot[:, pair * 2 * LANES : (pair + 1) * 2 * LANES])
            for i in range(2):
                x, y = (2 * pair + i) // WIDE, (2 * pair + i) % WIDE
                rank = rank_b[x, y]
                value = jnp.zeros((8, LANES), F32)
                for r in range(cap):
                    value = jnp.where(
                        rank == float(r),
                        both[8 * r : 8 * r + 8, i * LANES : (i + 1) * LANES],
                        value,
                    )
                coarse_field[target, x, y] = value

    def own_products(load, stack, rows, extra=None):
        def one(x, carry):
            for half in range(2):
                ys = (2 * half, 2 * half + 1)
                product = dot(stack[...], jnp.concatenate([load(x, y) for y in ys], axis=1))
                for i, y in enumerate(ys):

                    def block(b):
                        return product[b * rows : (b + 1) * rows, i * LANES : (i + 1) * LANES]

                    def scaled(weight, value):
                        return weight[None] * value.reshape(rows // 8, 8, LANES)

                    total = scaled(perm_b[x, y], block(0))
                    for d in range(6):
                        total = total + scaled(weights[d, x, y], block(1 + d))
                    total = total - scaled(weights[10, x, y], pltpu.roll(block(11), 1, 1))
                    total = total - scaled(weights[11, x, y], pltpu.roll(block(12), LANES - 1, 1))
                    acc[x, y, 0:rows, :] = total.reshape(rows, LANES)
                    gx0[x + 1, y, 0:rows, :] = block(7)
                    gx1[x, y, 0:rows, :] = block(8)
                    gy0[x, y + 1, 0:rows, :] = block(9)
                    gy1[x, y, 0:rows, :] = block(10)
                    if extra is not None:
                        extra(x, y, block(13))
            return carry

        lax.fori_loop(0, WIDE, one, 0)

    def halo_products(load, stack, rows):
        for side in range(4):
            data = jnp.concatenate([load(side, j) for j in range(WIDE)], axis=1)
            if rows == 64:
                product = dot(stack[(7 + side) * rows : (8 + side) * rows, :], data)
            else:
                product = dot(stack[...], data)[(7 + side) * rows : (8 + side) * rows]
            for j in range(WIDE):
                value = product[:, j * LANES : (j + 1) * LANES]
                if side == 0:
                    gx0[0, j, 0:rows, :] = value
                elif side == 1:
                    gx1[WIDE, j, 0:rows, :] = value
                elif side == 2:
                    gy0[j, 0, 0:rows, :] = value
                else:
                    gy1[j, WIDE, 0:rows, :] = value

    def applied(x, y, rows):
        def scaled(weight, value):
            return weight[None] * value.reshape(rows // 8, 8, LANES)

        total = acc[x, y, 0:rows, :].reshape(rows // 8, 8, LANES)
        total = total - scaled(weights[6, x, y], gx0[x, y, 0:rows, :])
        total = total - scaled(weights[7, x, y], gx1[x + 1, y, 0:rows, :])
        total = total - scaled(weights[8, x, y], gy0[x, y, 0:rows, :])
        total = total - scaled(weights[9, x, y], gy1[x, y + 1, 0:rows, :])
        return total.reshape(rows, LANES)

    def smoothed(values, labels, inverses):
        product = dot(smooth_stack[...], jnp.concatenate([stack_rows(v) for v in values], axis=1))
        results = []
        for i, (label, inverse) in enumerate(zip(labels, inverses)):
            columns = slice(i * LANES, (i + 1) * LANES)
            value = product[0:64, columns].reshape(8, 8, LANES)
            for k in range(1, 16):
                block = product[64 * k : 64 * k + 64, columns].reshape(8, 8, LANES)
                value = jnp.where((label == float(k))[None], block, value)
            results.append((value * inverse[None]).reshape(64, LANES))
        return results

    def label_of(x, y):
        return label[x, y]

    def first_sweep(x, carry):
        for half in range(2):
            ys = (2 * half, 2 * half + 1)
            found = smoothed(
                [rs[x, y] for y in ys],
                [label_of(x, y) for y in ys],
                [perm_inv[x, y] for y in ys],
            )
            for y, value in zip(ys, found):
                start_field[x, y] = value
        return carry

    lax.fori_loop(0, WIDE, first_sweep, 0)

    def keys(x, y):
        row = lax.broadcasted_iota(jnp.int32, (8, LANES), 0)
        label = jnp.broadcast_to(local_ref[pl.ds(x * WIDE + y, 1), :], (8, LANES)).astype(F32) + 1.0
        return jnp.where(row == 0, label, jnp.where(row == 1, perm_b[x, y], 0.0))

    pl.semaphore_wait(all_here, n_slab - 1)
    to_owner_start(0, keys)

    await_halo(label, halo_label, 6)
    inside = (s > 0, s < n_slab - 1, c > 0, c < n_cross - 1)
    for side in range(4):
        for j in range(WIDE):
            halo_coarse[0, side, j] = perm_of(halo_label[side, j])

    for x in range(WIDE):
        for y in range(WIDE):
            own = perm_b[x, y]

            def rim(side, j):
                return jnp.where(inside[side], halo_coarse[0, side, j], 0.0)

            beside = (
                perm_b[x - 1, y] if x > 0 else rim(0, y),
                perm_b[x + 1, y] if x < WIDE - 1 else rim(1, y),
                perm_b[x, y - 1] if y > 0 else rim(2, x),
                perm_b[x, y + 1] if y < WIDE - 1 else rim(3, x),
                jnp.where(lane > 0, pltpu.roll(own, 1, 1), 0.0),
                jnp.where(lane < LANES - 1, pltpu.roll(own, LANES - 1, 1), 0.0),
            )
            there = (
                True if x > 0 else inside[0],
                True if x < WIDE - 1 else inside[1],
                True if y > 0 else inside[2],
                True if y < WIDE - 1 else inside[3],
                lane > 0,
                lane < LANES - 1,
            )
            for d in range(6):
                kn = beside[d]
                w = jnp.where(kn > 0.0, 2.0 * own * kn / (own + kn), 2.0 * own)
                weights[d, x, y] = w
                weights[6 + d, x, y] = w if there[d] is True else jnp.where(there[d], w, 0.0)

    def fine_stack(ref, *lead):
        return lambda x, y: stack_rows(ref[(*lead, x, y)])

    own_products(fine_stack(start_field), op_stack, 64)

    await_halo(rs, halo_rhs, 0)

    def halo_sweep(side, carry):
        for half in range(2):
            js = (2 * half, 2 * half + 1)
            values = smoothed(
                [halo_rhs[side, j] for j in js],
                [halo_label[side, j] for j in js],
                [1.0 / halo_coarse[0, side, j] for j in js],
            )
            for j, value in zip(js, values):
                halos[3, side, j] = value
        return carry

    lax.fori_loop(0, 4, halo_sweep, 0)
    halo_products(fine_stack(halos, 3), op_stack, 64)

    def sweep(residue, iterate, target, turn):
        def one(step, carry):
            x = lax.rem(step * 3, WIDE)
            for half in range(2):
                ys = (2 * half, 2 * half + 1)
                found = smoothed(
                    [residue(x, y) for y in ys],
                    [label_of(x, y) for y in ys],
                    [perm_inv[x, y] for y in ys],
                )
                for y, value in zip(ys, found):
                    fields[target, x, y] = iterate(x, y) + value

            @pl.when(step == 0)
            def _():
                halo_copies(fields.at[target], halos.at[target], turn)[0].start()

            @pl.when(step == 1)
            def _():
                halo_copies(fields.at[target], halos.at[target], turn)[1].start()

            return carry

        lax.fori_loop(0, WIDE, one, 0)
        copies = halo_copies(fields.at[target], halos.at[target], turn)
        copies[2].start()
        copies[3].start()
        sent.extend(copy.wait_send for copy in copies)

    sweep(
        lambda x, y: rs[x, y] - applied(x, y, 64), lambda x, y: start_field[x, y], 0, 1
    )
    own_products(fine_stack(fields, 0), op_stack, 64)

    arrived = to_owner_end(0)
    hot_ids = lax.broadcasted_iota(jnp.int32, (LANES, owners), 0).astype(F32) + 1.0
    for r in range(cap):
        local_hot[:, r * owners : (r + 1) * owners] = jnp.where(
            hot_ids == arrived[8 * r : 8 * r + 1, :], 1.0, 0.0
        ).astype(BF16)
    perm_sum = gather_sum(arrived)[1:2, :]
    coarse_keep[0] = jnp.broadcast_to(1.0 / (1.0 + perm_sum), (8, LANES))

    await_halo(fields.at[0], halos.at[0], 1)
    halo_products(fine_stack(halos, 0), op_stack, 64)

    def second_residue(x, carry):
        rest = []
        for y in range(WIDE):
            value = rs[x, y] - applied(x, y, 64)
            fine_res[x, y] = value
            rest.append(stack_rows(value))
        found = dot(restrict_cols, jnp.concatenate(rest, axis=1))
        for y in range(WIDE):
            coarse_field[2, x, y] = found[0:8, y * LANES : (y + 1) * LANES]
        return carry

    lax.fori_loop(0, WIDE, second_residue, 0)

    def coarse_step(value):
        product = jnp.dot(
            coarse_ref[...], value, precision=HIGHEST, preferred_element_type=F32
        )
        return coarse_keep[0] * product

    to_owner_start(1, lambda x, y: coarse_field[2, x, y])
    coarse_res = gather_sum(to_owner_end(1))
    first = coarse_step(coarse_res)
    from_owner_start(3, first)
    from_owner_end(3, 0)
    send_halo(coarse_field.at[0], halo_coarse.at[1], 2)
    own_products(fine_stack(coarse_field, 0), coarse_stack, 8)
    await_halo(coarse_field.at[0], halo_coarse.at[1], 2)
    halo_products(fine_stack(halo_coarse, 1), coarse_stack, 8)
    to_owner_start(2, lambda x, y: applied(x, y, 8))
    again = coarse_res - gather_sum(to_owner_end(2))
    second = first + coarse_step(again)
    from_owner_start(4, second)
    from_owner_end(4, 1)
    send_halo(coarse_field.at[1], halo_coarse.at[2], 3)

    def add_prolonged(x, y, value):
        start_field[x, y] = fields[0, x, y] + value

    own_products(fine_stack(coarse_field, 1), prolong_stack, 64, add_prolonged)
    await_halo(coarse_field.at[1], halo_coarse.at[2], 3)
    halo_products(fine_stack(halo_coarse, 2), prolong_stack, 64)
    sweep(lambda x, y: fine_res[x, y] - applied(x, y, 64), lambda x, y: start_field[x, y], 1, 4)

    own_products(fine_stack(fields, 1), op_stack, 64)
    await_halo(fields.at[1], halos.at[1], 4)
    halo_products(fine_stack(halos, 1), op_stack, 64)
    sweep(
        lambda x, y: rs[x, y] - applied(x, y, 64), lambda x, y: fields[1, x, y], 2, 5
    )
    own_products(fine_stack(fields, 2), op_stack, 64)
    for xy in range(WIDE * WIDE):
        sol_ref[pl.ds(xy, 64, stride=WIDE * WIDE), :] = fields[2, xy // WIDE, xy % WIDE]
    await_halo(fields.at[2], halos.at[2], 5)
    halo_products(fine_stack(halos, 2), op_stack, 64)
    for xy in range(WIDE * WIDE):
        x, y = xy // WIDE, xy % WIDE
        res_ref[pl.ds(xy, 64, stride=WIDE * WIDE), :] = rs[x, y] - applied(x, y, 64)

    drain()


def hand_over(sol_in, res_in, sol_out, res_out, sem):
    copies = [
        pltpu.make_async_copy(sol_in, sol_out, sem.at[0]),
        pltpu.make_async_copy(res_in, res_out, sem.at[1]),
    ]
    for copy in copies:
        copy.start()
    for copy in copies:
        copy.wait()


def local(
    n_slab,
    n_cross,
    cap,
    rhs,
    classes,
    perm,
    vol_block,
    side_blocks,
    couple,
    smoother_blocks,
    restrict_map,
    coarse_block,
    owners,
    agg_local,
):
    anywhere = pl.BlockSpec(memory_space=pl.ANY)
    count = n_slab * n_cross
    face = (WIDE, WIDE)
    flat = jax.ShapeDtypeStruct((64 * WIDE * WIDE, LANES), F32)
    scratch = [
        pltpu.VMEM((64 * WIDE * WIDE, LANES), F32),
        pltpu.VMEM((WIDE * WIDE, LANES), jnp.int32),
        pltpu.SMEM((16,), F32),
        pltpu.VMEM((64, 64), F32),
        pltpu.VMEM((6 * 64, 64), F32),
        pltpu.VMEM((3 * 64, 64), F32),
        pltpu.VMEM((16 * 64, 64), F32),
        pltpu.VMEM((8, 64), F32),
        pltpu.VMEM((8, 8), F32),
        pltpu.VMEM((WIDE * WIDE, LANES), jnp.int32),
        pltpu.VMEM((WIDE * WIDE, LANES), jnp.int32),
        pltpu.VMEM((*face, 64, LANES), F32),
        pltpu.VMEM((4, WIDE, 64, LANES), F32),
        pltpu.VMEM((*face, 8, LANES), F32),
        pltpu.VMEM((4, WIDE, 8, LANES), F32),
        pltpu.VMEM((3, *face, 64, LANES), F32),
        pltpu.VMEM((4, 4, WIDE, 64, LANES), F32),
        pltpu.VMEM((*face, 64, LANES), F32),
        pltpu.VMEM((*face, 64, LANES), F32),
        pltpu.VMEM((*face, 64, LANES), F32),
        pltpu.VMEM((WIDE + 1, WIDE, 64, LANES), F32),
        pltpu.VMEM((WIDE + 1, WIDE, 64, LANES), F32),
        pltpu.VMEM((WIDE, WIDE + 1, 64, LANES), F32),
        pltpu.VMEM((WIDE, WIDE + 1, 64, LANES), F32),
        pltpu.VMEM((14 * 64, 64), F32),
        pltpu.VMEM((13 * 64, 192), BF16),
        pltpu.VMEM((16 * 64, 192), BF16),
        pltpu.VMEM((14 * 64, 32), BF16),
        pltpu.VMEM((14 * 8, 32), BF16),
        pltpu.VMEM((*face, 8, LANES), F32),
        pltpu.VMEM((*face, 8, LANES), F32),
        pltpu.VMEM((12, *face, 8, LANES), F32),
        pltpu.VMEM((2 * count, WIDE * WIDE * LANES), BF16),
        pltpu.VMEM((*face, 8, LANES), F32),
        pltpu.VMEM((2 * cap * 8, WIDE * WIDE * LANES), BF16),
        pltpu.VMEM((LANES, cap * count), BF16),
        pltpu.VMEM((5, 2, count, cap // 16, LANES), F32),
        pltpu.VMEM((1, 8, LANES), F32),
        pltpu.VMEM((3, *face, 8, LANES), F32),
        pltpu.VMEM((3, 4, WIDE, 8, LANES), F32),
        pltpu.SemaphoreType.DMA((11,)),
        pltpu.SemaphoreType.DMA((7, 4)),
        pltpu.SemaphoreType.DMA((7, 4)),
        pltpu.SemaphoreType.DMA((5,)),
        pltpu.SemaphoreType.DMA((5,)),
        pltpu.SemaphoreType.REGULAR,
    ]
    flops = 2 * 2048 * (5 * 832 + 5 * 1024) * 192
    kept = pltpu.VMEM(flat.shape, F32)
    vmem = pl.BlockSpec(memory_space=pltpu.VMEM)
    arguments = (
        rhs.reshape(64 * WIDE * WIDE, LANES),
        classes.reshape(WIDE * WIDE, LANES),
        perm,
        vol_block,
        side_blocks.reshape(6 * 64, 64),
        couple.reshape(3 * 64, 64),
        smoother_blocks.reshape(16 * 64, 64),
        restrict_map,
        coarse_block,
        owners.reshape(WIDE * WIDE, LANES),
        agg_local.reshape(WIDE * WIDE, LANES),
    )
    solved, residue = pl.pallas_call(
        functools.partial(cycle, n_slab, n_cross, cap),
        out_shape=(kept, kept),
        in_specs=[pl.BlockSpec(memory_space=pltpu.HBM)] * 11,
        out_specs=(vmem, vmem),
        scratch_shapes=scratch,
        compiler_params=pltpu.CompilerParams(
            collective_id=0, has_side_effects=True, vmem_limit_bytes=40 * 1024 * 1024
        ),
        cost_estimate=pl.CostEstimate(flops=flops, bytes_accessed=4 << 20, transcendentals=0),
    )(*(pltpu.with_memory_space_constraint(value, pltpu.HBM) for value in arguments))
    solved, residue = pl.pallas_call(
        hand_over,
        out_shape=(flat, flat),
        in_specs=[vmem, vmem],
        out_specs=(anywhere, anywhere),
        scratch_shapes=[pltpu.SemaphoreType.DMA((2,))],
    )(solved, residue)
    return solved.reshape(rhs.shape), residue.reshape(rhs.shape)


def solution(mesh, cap=32):
    placed = (
        P(None, "slab", "cross", None),
        P("slab", "cross", None),
        P(),
        P(),
        P(),
        P(),
        P(),
        P(),
        P(),
        P("slab", "cross", None, None),
        P("slab", "cross", None),
    )
    return jax.shard_map(
        functools.partial(local, mesh.shape["slab"], mesh.shape["cross"], cap),
        mesh=mesh,
        in_specs=placed,
        out_specs=(P(None, "slab", "cross", None), P(None, "slab", "cross", None)),
        check_vma=False,
    )
```

```python
import functools

import jax
import jax.numpy as jnp
from jax import lax
from jax.experimental import pallas as pl
from jax.experimental.pallas import tpu as pltpu
from jax.sharding import PartitionSpec as P

MESH = pl.DeviceIdType.MESH
F32 = jnp.float32
BF16 = jnp.bfloat16
HIGHEST = lax.Precision.HIGHEST
LANES = 128
WIDE = 4
NT = (((1,), (1,)), ((), ()))


def dot(a, b):
    return jnp.dot(a, b, preferred_element_type=F32)


def dot_nt(a, b):
    return lax.dot_general(a, b, NT, preferred_element_type=F32)


def parts(value):
    high = value.astype(BF16).astype(F32)
    return high, value - high


def stack_rows(value):
    high, low = parts(value)
    pieces = [high, low, high]
    if value.shape[0] == 8:
        pieces.append(jnp.zeros_like(value))
    return jnp.concatenate(pieces, axis=0).astype(BF16)


def stack_columns(value):
    high, low = parts(value)
    pieces = [high, high, low]
    if value.shape[1] == 8:
        pieces.append(jnp.zeros_like(value))
    return jnp.concatenate(pieces, axis=1).astype(BF16)


def cycle(
    n_slab,
    n_cross,
    cap,
    rhs_hbm,
    class_hbm,
    perm_hbm,
    vol_hbm,
    side_hbm,
    couple_hbm,
    smooth_hbm,
    restrict_hbm,
    coarse_hbm,
    owner_hbm,
    local_hbm,
    sol_ref,
    res_ref,
    rhs_ref,
    class_ref,
    perm_ref,
    vol_ref,
    side_ref,
    couple_ref,
    smooth_ref,
    restrict_ref,
    coarse_ref,
    owner_ref,
    local_ref,
    rs,
    label,
    halo_label,
    fields,
    halos,
    start_field,
    fine_res,
    acc,
    gx0,
    gx1,
    gy0,
    gy1,
    blocks_f32,
    op_stack,
    smooth_stack,
    prolong_stack,
    coarse_stack,
    perm_b,
    perm_inv,
    weights,
    owner_hot,
    rank_b,
    packed,
    local_hot,
    mail,
    coarse_keep,
    coarse_field,
    halo_coarse,
    load_sem,
    halo_send,
    halo_recv,
    mail_send,
    mail_recv,
    all_here,
):
    s, c = lax.axis_index("slab"), lax.axis_index("cross")
    owners = n_slab * n_cross
    s_up, s_down = lax.rem(s + 1, n_slab), lax.rem(s + n_slab - 1, n_slab)
    c_up, c_down = lax.rem(c + 1, n_cross), lax.rem(c + n_cross - 1, n_cross)
    lane = lax.broadcasted_iota(jnp.int32, (8, LANES), 1)

    barrier = pltpu.get_barrier_semaphore()

    def greet_slab(off, carry):
        pl.semaphore_signal(
            barrier, inc=1, device_id=(lax.rem(s + off, n_slab), c), device_id_type=MESH
        )
        return carry

    def greet_cross(off, carry):
        pl.semaphore_signal(
            barrier, inc=1, device_id=(s, lax.rem(c + off, n_cross)), device_id_type=MESH
        )
        return carry

    lax.fori_loop(1, n_slab, greet_slab, 0)
    lax.fori_loop(1, n_cross, greet_cross, 0)

    loads = [
        pltpu.make_async_copy(source, target, load_sem.at[k])
        for k, (source, target) in enumerate(
            (
                (rhs_hbm, rhs_ref),
                (class_hbm, class_ref),
                (perm_hbm, perm_ref),
                (vol_hbm, vol_ref),
                (side_hbm, side_ref),
                (couple_hbm, couple_ref),
                (smooth_hbm, smooth_ref),
                (restrict_hbm, restrict_ref),
                (coarse_hbm, coarse_ref),
                (owner_hbm, owner_ref),
                (local_hbm, local_ref),
            )
        )
    ]
    for copy in loads:
        copy.start()
    for k in (0, 1, 2, 6):
        loads[k].wait()

    for xy in range(WIDE * WIDE):
        x, y = xy // WIDE, xy % WIDE
        rs[x, y] = rhs_ref[pl.ds(xy, 64, stride=WIDE * WIDE), :]
        label[x, y] = jnp.broadcast_to(class_ref[xy : xy + 1, :], (8, LANES)).astype(F32)

    sent = []

    def drain():
        for finish in sent:
            finish()

    def halo_copies(source, target, turn):
        plan = (
            (source.at[0], 1, (s_down, c)),
            (source.at[WIDE - 1], 0, (s_up, c)),
            (source.at[:, 0], 3, (s, c_down)),
            (source.at[:, WIDE - 1], 2, (s, c_up)),
        )
        return [
            pltpu.make_async_remote_copy(
                src_ref=face,
                dst_ref=target.at[side],
                send_sem=halo_send.at[turn, side],
                recv_sem=halo_recv.at[turn, side],
                device_id=device,
                device_id_type=MESH,
            )
            for face, side, device in plan
        ]

    def send_halo(source, target, turn):
        for copy in halo_copies(source, target, turn):
            copy.start()
            sent.append(copy.wait_send)

    def await_halo(source, target, turn):
        for copy in halo_copies(source, target, turn):
            copy.wait_recv()

    def perm_of(kind):
        value = jnp.zeros_like(kind)
        for k in range(16):
            value = jnp.where(kind == float(k), perm_ref[k], value)
        return value

    def own_perm(x, carry):
        for y in range(WIDE):
            value = perm_of(label[x, y])
            perm_b[x, y] = value
            perm_inv[x, y] = 1.0 / value
        return carry

    lax.fori_loop(0, WIDE, own_perm, 0)

    for m in range(16):
        rows = slice(64 * m, 64 * m + 64)
        smooth_stack[rows, :] = stack_columns(smooth_ref[rows, :])

    def smoothed(values, labels, inverses):
        product = dot(smooth_stack[...], jnp.concatenate([stack_rows(v) for v in values], axis=1))
        results = []
        for i, (label, inverse) in enumerate(zip(labels, inverses)):
            columns = slice(i * LANES, (i + 1) * LANES)
            value = product[0:64, columns].reshape(8, 8, LANES)
            for k in range(1, 16):
                block = product[64 * k : 64 * k + 64, columns].reshape(8, 8, LANES)
                value = jnp.where((label == float(k))[None], block, value)
            results.append((value * inverse[None]).reshape(64, LANES))
        return results

    def label_of(x, y):
        return label[x, y]

    def first_sweep(step, carry):
        x = lax.rem(step * 3, WIDE)
        for half in range(2):
            ys = (2 * half, 2 * half + 1)
            found = smoothed(
                [rs[x, y] for y in ys],
                [label_of(x, y) for y in ys],
                [perm_inv[x, y] for y in ys],
            )
            for y, value in zip(ys, found):
                start_field[x, y] = value
        return carry

    lax.fori_loop(0, 2, first_sweep, 0)
    pl.semaphore_wait(barrier, n_slab + n_cross - 2)
    send_halo(label, halo_label, 6)
    first_copies = halo_copies(start_field, halos.at[3], 0)
    first_copies[0].start()
    first_copies[1].start()
    lax.fori_loop(2, WIDE, first_sweep, 0)
    first_copies[2].start()
    first_copies[3].start()
    sent.extend(copy.wait_send for copy in first_copies)
    for k in (3, 4, 5, 7, 8, 9, 10):
        loads[k].wait()

    def greet_again(off, carry):
        pl.semaphore_signal(
            all_here, inc=1, device_id=(lax.rem(s + off, n_slab), c), device_id_type=MESH
        )
        return carry

    lax.fori_loop(1, n_slab, greet_again, 0)

    blocks_f32[0:64, :] = vol_ref[...]
    blocks_f32[64:448, :] = side_ref[...]
    for m in range(3):
        plus = couple_ref[m * 64 : (m + 1) * 64, :]
        blocks_f32[448 + 128 * m : 512 + 128 * m, :] = plus.T
        blocks_f32[512 + 128 * m : 576 + 128 * m, :] = plus
    blocks_f32[832:896, :] = jnp.where(
        lax.broadcasted_iota(jnp.int32, (64, 64), 0) == lax.broadcasted_iota(jnp.int32, (64, 64), 1),
        1.0,
        0.0,
    )
    for m in range(13):
        rows = slice(64 * m, 64 * m + 64)
        op_stack[rows, :] = stack_columns(blocks_f32[rows, :])
    restrict = restrict_ref[...]
    short = lax.dot_general(
        blocks_f32[...], restrict, NT, precision=HIGHEST, preferred_element_type=F32
    )
    prolong_stack[...] = stack_columns(short)
    tiny = [
        jnp.dot(restrict, short[64 * m : 64 * m + 64], precision=HIGHEST, preferred_element_type=F32)
        for m in range(13)
    ]
    coarse_stack[...] = stack_columns(jnp.concatenate(tiny + [jnp.zeros((8, 8), F32)], axis=0))
    restrict_cols = stack_columns(jnp.concatenate([restrict, jnp.zeros_like(restrict)], axis=0))

    hot_rows = lax.broadcasted_iota(jnp.int32, (owners, LANES), 0)
    before = jnp.concatenate(
        [
            jnp.where(
                lax.broadcasted_iota(jnp.int32, (LANES, LANES), 0)
                < lax.broadcasted_iota(jnp.int32, (LANES, LANES), 1),
                1.0,
                0.0,
            ),
            jnp.ones((LANES, LANES), F32),
        ],
        axis=1,
    ).astype(BF16)
    seen = jnp.zeros((owners, LANES), F32)
    for xy in range(WIDE * WIDE):
        x, y = xy // WIDE, xy % WIDE
        hot = jnp.where(hot_rows == owner_ref[xy : xy + 1, :], 1.0, 0.0)
        hot_low = hot.astype(BF16)
        owner_hot[0:owners, xy * LANES : (xy + 1) * LANES] = hot_low
        owner_hot[owners : 2 * owners, xy * LANES : (xy + 1) * LANES] = hot_low
        counted = dot(hot_low, before)
        rank = jnp.sum(hot * (counted[:, 0:LANES] + seen), axis=0, keepdims=True)
        seen = seen + counted[:, LANES : 2 * LANES]
        rank_b[x, y] = jnp.broadcast_to(rank, (8, LANES))

    side_y = WIDE
    side_x = n_slab // side_y
    me = s * n_cross + c
    s_x, s_y = s // side_y, lax.rem(s, side_y)

    def hops(step):
        return min(step[0], side_x - step[0]) + min(step[1], side_y - step[1])

    far_first = sorted(
        ((i, j) for i in range(side_x) for j in range(side_y)), key=lambda step: -hops(step)
    )

    def post(turn):
        for step in far_first:
            to_slab = lax.rem(s_x + step[0], side_x) * side_y + lax.rem(s_y + step[1], side_y)

            def one(off, carry):
                to_cross = lax.rem(c + off, n_cross)
                pltpu.make_async_remote_copy(
                    src_ref=mail.at[turn, 0, to_slab * n_cross + to_cross],
                    dst_ref=mail.at[turn, 1, me],
                    send_sem=mail_send.at[turn],
                    recv_sem=mail_recv.at[turn],
                    device_id=(to_slab, to_cross),
                    device_id_type=MESH,
                ).start()
                return carry

            lax.fori_loop(0 if hops(step) else 1, n_cross, one, 0, unroll=True)
        sent.append(functools.partial(release, turn))
        mail[turn, 1, me] = mail[turn, 0, me]

    def collect(turn):
        part = mail.at[turn, 1, pl.ds(0, owners - 1)]
        pltpu.make_async_copy(part, part, mail_recv.at[turn]).wait()

    def release(turn):
        part = mail.at[turn, 0, pl.ds(0, owners - 1)]
        pltpu.make_async_copy(part, part, mail_send.at[turn]).wait()

    def write_mail(turn, value):
        mail[turn, 0] = value.reshape(owners, cap // 16, LANES)

    def read_mail(turn):
        return mail[turn, 1].reshape(owners, cap * 8).T

    def pack(load):
        def one(x, carry):
            for y in range(WIDE):
                rank = rank_b[x, y]
                keep = [rank == float(r) for r in range(cap)]
                columns = pl.ds(pl.multiple_of((x * WIDE + y) * LANES, LANES), LANES)
                for i, piece in enumerate(parts(load(x, y))):
                    spread = jnp.concatenate([jnp.where(k, piece, 0.0) for k in keep], axis=0)
                    packed[i * cap * 8 : (i + 1) * cap * 8, columns] = spread.astype(BF16)
            return carry

        lax.fori_loop(0, WIDE, one, 0)

    def to_owner_start(turn, load):
        pack(load)
        slots = dot_nt(owner_hot[0:owners, :], packed[...])
        write_mail(turn, slots[:, 0 : cap * 8] + slots[:, cap * 8 : 2 * cap * 8])
        post(turn)

    def to_owner_end(turn):
        collect(turn)
        return read_mail(turn)

    def gather_sum(arrived):
        flat = jnp.concatenate([arrived[8 * r : 8 * r + 8] for r in range(cap)], axis=1)
        high, low = parts(flat)
        both = dot_nt(jnp.concatenate([high, low], axis=0).astype(BF16), local_hot[...])
        return both[0:8] + both[8:16]

    def from_owner_start(turn, value):
        high, low = parts(value)
        both = dot(jnp.concatenate([high, low], axis=0).astype(BF16), local_hot[...])
        flat = both[0:8] + both[8:16]
        out = jnp.concatenate([flat[:, owners * r : owners * (r + 1)] for r in range(cap)], axis=0)
        write_mail(turn, out.T)
        post(turn)

    def from_owner_end(turn, target):
        collect(turn)
        high, low = parts(read_mail(turn))
        spread = jnp.concatenate([high, low], axis=1).astype(BF16)
        for pair in range(WIDE * WIDE // 2):
            both = dot(spread, owner_hot[:, pair * 2 * LANES : (pair + 1) * 2 * LANES])
            for i in range(2):
                x, y = (2 * pair + i) // WIDE, (2 * pair + i) % WIDE
                rank = rank_b[x, y]
                value = jnp.zeros((8, LANES), F32)
                for r in range(cap):
                    value = jnp.where(
                        rank == float(r),
                        both[8 * r : 8 * r + 8, i * LANES : (i + 1) * LANES],
                        value,
                    )
                coarse_field[target, x, y] = value

    def own_products(load, stack, rows, extra=None):
        def one(x, carry):
            for half in range(2):
                ys = (2 * half, 2 * half + 1)
                product = dot(stack[...], jnp.concatenate([load(x, y) for y in ys], axis=1))
                for i, y in enumerate(ys):

                    def block(b):
                        return product[b * rows : (b + 1) * rows, i * LANES : (i + 1) * LANES]

                    def scaled(weight, value):
                        return weight[None] * value.reshape(rows // 8, 8, LANES)

                    total = scaled(perm_b[x, y], block(0))
                    for d in range(6):
                        total = total + scaled(weights[d, x, y], block(1 + d))
                    total = total - scaled(weights[10, x, y], pltpu.roll(block(11), 1, 1))
                    total = total - scaled(weights[11, x, y], pltpu.roll(block(12), LANES - 1, 1))
                    acc[x, y, 0:rows, :] = total.reshape(rows, LANES)
                    gx0[x + 1, y, 0:rows, :] = block(7)
                    gx1[x, y, 0:rows, :] = block(8)
                    gy0[x, y + 1, 0:rows, :] = block(9)
                    gy1[x, y, 0:rows, :] = block(10)
                    if extra is not None:
                        extra(x, y, block(13))
            return carry

        lax.fori_loop(0, WIDE, one, 0)

    def halo_products(load, stack, rows):
        for side in range(4):
            data = jnp.concatenate([load(side, j) for j in range(WIDE)], axis=1)
            if rows == 64:
                product = dot(stack[(7 + side) * rows : (8 + side) * rows, :], data)
            else:
                product = dot(stack[...], data)[(7 + side) * rows : (8 + side) * rows]
            for j in range(WIDE):
                value = product[:, j * LANES : (j + 1) * LANES]
                if side == 0:
                    gx0[0, j, 0:rows, :] = value
                elif side == 1:
                    gx1[WIDE, j, 0:rows, :] = value
                elif side == 2:
                    gy0[j, 0, 0:rows, :] = value
                else:
                    gy1[j, WIDE, 0:rows, :] = value

    def applied(x, y, rows):
        def scaled(weight, value):
            return weight[None] * value.reshape(rows // 8, 8, LANES)

        total = acc[x, y, 0:rows, :].reshape(rows // 8, 8, LANES)
        total = total - scaled(weights[6, x, y], gx0[x, y, 0:rows, :])
        total = total - scaled(weights[7, x, y], gx1[x + 1, y, 0:rows, :])
        total = total - scaled(weights[8, x, y], gy0[x, y, 0:rows, :])
        total = total - scaled(weights[9, x, y], gy1[x, y + 1, 0:rows, :])
        return total.reshape(rows, LANES)

    await_halo(label, halo_label, 6)
    inside = (s > 0, s < n_slab - 1, c > 0, c < n_cross - 1)
    for side in range(4):
        for j in range(WIDE):
            halo_coarse[0, side, j] = perm_of(halo_label[side, j])

    for x in range(WIDE):
        for y in range(WIDE):
            own = perm_b[x, y]

            def rim(side, j):
                return jnp.where(inside[side], halo_coarse[0, side, j], 0.0)

            beside = (
                perm_b[x - 1, y] if x > 0 else rim(0, y),
                perm_b[x + 1, y] if x < WIDE - 1 else rim(1, y),
                perm_b[x, y - 1] if y > 0 else rim(2, x),
                perm_b[x, y + 1] if y < WIDE - 1 else rim(3, x),
                jnp.where(lane > 0, pltpu.roll(own, 1, 1), 0.0),
                jnp.where(lane < LANES - 1, pltpu.roll(own, LANES - 1, 1), 0.0),
            )
            there = (
                True if x > 0 else inside[0],
                True if x < WIDE - 1 else inside[1],
                True if y > 0 else inside[2],
                True if y < WIDE - 1 else inside[3],
                lane > 0,
                lane < LANES - 1,
            )
            for d in range(6):
                kn = beside[d]
                w = jnp.where(kn > 0.0, 2.0 * own * kn / (own + kn), 2.0 * own)
                weights[d, x, y] = w
                weights[6 + d, x, y] = w if there[d] is True else jnp.where(there[d], w, 0.0)

    def fine_stack(ref, *lead):
        return lambda x, y: stack_rows(ref[(*lead, x, y)])

    own_products(fine_stack(start_field), op_stack, 64)

    await_halo(start_field, halos.at[3], 0)
    halo_products(fine_stack(halos, 3), op_stack, 64)

    def sweep(residue, iterate, target, turn):
        def one(step, carry):
            x = lax.rem(step * 3, WIDE)
            for half in range(2):
                ys = (2 * half, 2 * half + 1)
                found = smoothed(
                    [residue(x, y) for y in ys],
                    [label_of(x, y) for y in ys],
                    [perm_inv[x, y] for y in ys],
                )
                for y, value in zip(ys, found):
                    fields[target, x, y] = iterate(x, y) + value

            @pl.when(step == 0)
            def _():
                halo_copies(fields.at[target], halos.at[target], turn)[0].start()

            @pl.when(step == 1)
            def _():
                halo_copies(fields.at[target], halos.at[target], turn)[1].start()

            return carry

        lax.fori_loop(0, WIDE, one, 0)
        copies = halo_copies(fields.at[target], halos.at[target], turn)
        copies[2].start()
        copies[3].start()
        sent.extend(copy.wait_send for copy in copies)

    sweep(
        lambda x, y: rs[x, y] - applied(x, y, 64), lambda x, y: start_field[x, y], 0, 1
    )
    own_products(fine_stack(fields, 0), op_stack, 64)

    def keys(x, y):
        row = lax.broadcasted_iota(jnp.int32, (8, LANES), 0)
        label = jnp.broadcast_to(local_ref[pl.ds(x * WIDE + y, 1), :], (8, LANES)).astype(F32) + 1.0
        return jnp.where(row == 0, label, jnp.where(row == 1, perm_b[x, y], 0.0))

    pl.semaphore_wait(all_here, n_slab - 1)
    to_owner_start(0, keys)

    await_halo(fields.at[0], halos.at[0], 1)
    halo_products(fine_stack(halos, 0), op_stack, 64)

    def second_residue(x, carry):
        rest = []
        for y in range(WIDE):
            value = rs[x, y] - applied(x, y, 64)
            fine_res[x, y] = value
            rest.append(stack_rows(value))
        found = dot(restrict_cols, jnp.concatenate(rest, axis=1))
        for y in range(WIDE):
            coarse_field[2, x, y] = found[0:8, y * LANES : (y + 1) * LANES]
        return carry

    lax.fori_loop(0, WIDE, second_residue, 0)

    def coarse_step(value):
        product = jnp.dot(
            coarse_ref[...], value, precision=HIGHEST, preferred_element_type=F32
        )
        return coarse_keep[0] * product

    to_owner_start(1, lambda x, y: coarse_field[2, x, y])
    arrived = to_owner_end(0)
    hot_ids = lax.broadcasted_iota(jnp.int32, (LANES, owners), 0).astype(F32) + 1.0
    for r in range(cap):
        local_hot[:, r * owners : (r + 1) * owners] = jnp.where(
            hot_ids == arrived[8 * r : 8 * r + 1, :], 1.0, 0.0
        ).astype(BF16)
    perm_sum = gather_sum(arrived)[1:2, :]
    coarse_keep[0] = jnp.broadcast_to(1.0 / (1.0 + perm_sum), (8, LANES))

    coarse_res = gather_sum(to_owner_end(1))
    first = coarse_step(coarse_res)
    from_owner_start(3, first)
    from_owner_end(3, 0)
    send_halo(coarse_field.at[0], halo_coarse.at[1], 2)
    own_products(fine_stack(coarse_field, 0), coarse_stack, 8)
    await_halo(coarse_field.at[0], halo_coarse.at[1], 2)
    halo_products(fine_stack(halo_coarse, 1), coarse_stack, 8)
    to_owner_start(2, lambda x, y: applied(x, y, 8))
    again = coarse_res - gather_sum(to_owner_end(2))
    second = first + coarse_step(again)
    from_owner_start(4, second)
    from_owner_end(4, 1)
    send_halo(coarse_field.at[1], halo_coarse.at[2], 3)

    def add_prolonged(x, y, value):
        fields[3, x, y] = fields[0, x, y] + value

    own_products(fine_stack(coarse_field, 1), prolong_stack, 64, add_prolonged)
    await_halo(coarse_field.at[1], halo_coarse.at[2], 3)
    halo_products(fine_stack(halo_coarse, 2), prolong_stack, 64)
    sweep(lambda x, y: fine_res[x, y] - applied(x, y, 64), lambda x, y: fields[3, x, y], 1, 4)

    own_products(fine_stack(fields, 1), op_stack, 64)
    await_halo(fields.at[1], halos.at[1], 4)
    halo_products(fine_stack(halos, 1), op_stack, 64)
    sweep(
        lambda x, y: rs[x, y] - applied(x, y, 64), lambda x, y: fields[1, x, y], 2, 5
    )
    own_products(fine_stack(fields, 2), op_stack, 64)
    for xy in range(WIDE * WIDE):
        sol_ref[pl.ds(xy, 64, stride=WIDE * WIDE), :] = fields[2, xy // WIDE, xy % WIDE]
    await_halo(fields.at[2], halos.at[2], 5)
    halo_products(fine_stack(halos, 2), op_stack, 64)
    for xy in range(WIDE * WIDE):
        x, y = xy // WIDE, xy % WIDE
        res_ref[pl.ds(xy, 64, stride=WIDE * WIDE), :] = rs[x, y] - applied(x, y, 64)

    drain()


def hand_over(sol_in, res_in, sol_out, res_out, sem):
    rows = sol_in.shape[0] // 4
    copies = [
        pltpu.make_async_copy(
            source.at[pl.ds(k * rows, rows)], target.at[pl.ds(k * rows, rows)], sem.at[i, k]
        )
        for i, (source, target) in enumerate(((sol_in, sol_out), (res_in, res_out)))
        for k in range(4)
    ]
    for copy in copies:
        copy.start()
    for copy in copies:
        copy.wait()


def local(
    n_slab,
    n_cross,
    cap,
    rhs,
    classes,
    perm,
    vol_block,
    side_blocks,
    couple,
    smoother_blocks,
    restrict_map,
    coarse_block,
    owners,
    agg_local,
):
    count = n_slab * n_cross
    face = (WIDE, WIDE)
    flat = jax.ShapeDtypeStruct((64 * WIDE * WIDE, LANES), F32)
    scratch = [
        pltpu.VMEM((64 * WIDE * WIDE, LANES), F32),
        pltpu.VMEM((WIDE * WIDE, LANES), jnp.int32),
        pltpu.SMEM((16,), F32),
        pltpu.VMEM((64, 64), F32),
        pltpu.VMEM((6 * 64, 64), F32),
        pltpu.VMEM((3 * 64, 64), F32),
        pltpu.VMEM((16 * 64, 64), F32),
        pltpu.VMEM((8, 64), F32),
        pltpu.VMEM((8, 8), F32),
        pltpu.VMEM((WIDE * WIDE, LANES), jnp.int32),
        pltpu.VMEM((WIDE * WIDE, LANES), jnp.int32),
        pltpu.VMEM((*face, 64, LANES), F32),
        pltpu.VMEM((*face, 8, LANES), F32),
        pltpu.VMEM((4, WIDE, 8, LANES), F32),
        pltpu.VMEM((4, *face, 64, LANES), F32),
        pltpu.VMEM((4, 4, WIDE, 64, LANES), F32),
        pltpu.VMEM((*face, 64, LANES), F32),
        pltpu.VMEM((*face, 64, LANES), F32),
        pltpu.VMEM((*face, 64, LANES), F32),
        pltpu.VMEM((WIDE + 1, WIDE, 64, LANES), F32),
        pltpu.VMEM((WIDE + 1, WIDE, 64, LANES), F32),
        pltpu.VMEM((WIDE, WIDE + 1, 64, LANES), F32),
        pltpu.VMEM((WIDE, WIDE + 1, 64, LANES), F32),
        pltpu.VMEM((14 * 64, 64), F32),
        pltpu.VMEM((13 * 64, 192), BF16),
        pltpu.VMEM((16 * 64, 192), BF16),
        pltpu.VMEM((14 * 64, 32), BF16),
        pltpu.VMEM((14 * 8, 32), BF16),
        pltpu.VMEM((*face, 8, LANES), F32),
        pltpu.VMEM((*face, 8, LANES), F32),
        pltpu.VMEM((12, *face, 8, LANES), F32),
        pltpu.VMEM((2 * count, WIDE * WIDE * LANES), BF16),
        pltpu.VMEM((*face, 8, LANES), F32),
        pltpu.VMEM((2 * cap * 8, WIDE * WIDE * LANES), BF16),
        pltpu.VMEM((LANES, cap * count), BF16),
        pltpu.VMEM((5, 2, count, cap // 16, LANES), F32),
        pltpu.VMEM((1, 8, LANES), F32),
        pltpu.VMEM((3, *face, 8, LANES), F32),
        pltpu.VMEM((3, 4, WIDE, 8, LANES), F32),
        pltpu.SemaphoreType.DMA((11,)),
        pltpu.SemaphoreType.DMA((7, 4)),
        pltpu.SemaphoreType.DMA((7, 4)),
        pltpu.SemaphoreType.DMA((5,)),
        pltpu.SemaphoreType.DMA((5,)),
        pltpu.SemaphoreType.REGULAR,
    ]
    flops = 2 * 2048 * (5 * 832 + 5 * 1024) * 192
    kept = pltpu.VMEM(flat.shape, F32)
    vmem = pl.BlockSpec(memory_space=pltpu.VMEM)
    arguments = (
        rhs.reshape(64 * WIDE * WIDE, LANES),
        classes.reshape(WIDE * WIDE, LANES),
        perm,
        vol_block,
        side_blocks.reshape(6 * 64, 64),
        couple.reshape(3 * 64, 64),
        smoother_blocks.reshape(16 * 64, 64),
        restrict_map,
        coarse_block,
        owners.reshape(WIDE * WIDE, LANES),
        agg_local.reshape(WIDE * WIDE, LANES),
    )
    solved, residue = pl.pallas_call(
        functools.partial(cycle, n_slab, n_cross, cap),
        out_shape=(kept, kept),
        in_specs=[pl.BlockSpec(memory_space=pltpu.HBM)] * 11,
        out_specs=(vmem, vmem),
        scratch_shapes=scratch,
        compiler_params=pltpu.CompilerParams(
            collective_id=0, has_side_effects=True, vmem_limit_bytes=40 * 1024 * 1024
        ),
        cost_estimate=pl.CostEstimate(flops=flops, bytes_accessed=4 << 20, transcendentals=0),
    )(*(pltpu.with_memory_space_constraint(value, pltpu.HBM) for value in arguments))
    solved, residue = pl.pallas_call(
        hand_over,
        out_shape=(pltpu.HBM(flat.shape, F32),) * 2,
        in_specs=[vmem, vmem],
        out_specs=(pl.BlockSpec(memory_space=pltpu.HBM),) * 2,
        scratch_shapes=[pltpu.SemaphoreType.DMA((2, 4))],
    )(solved, residue)
    return solved.reshape(rhs.shape), residue.reshape(rhs.shape)


def solution(mesh, cap=32):
    placed = (
        P(None, "slab", "cross", None),
        P("slab", "cross", None),
        P(),
        P(),
        P(),
        P(),
        P(),
        P(),
        P(),
        P("slab", "cross", None, None),
        P("slab", "cross", None),
    )
    return jax.shard_map(
        functools.partial(local, mesh.shape["slab"], mesh.shape["cross"], cap),
        mesh=mesh,
        in_specs=placed,
        out_specs=(P(None, "slab", "cross", None), P(None, "slab", "cross", None)),
        check_vma=False,
    )
```

```python
import functools

import jax
import jax.numpy as jnp
from jax import lax
from jax.experimental import pallas as pl
from jax.experimental.pallas import tpu as pltpu
from jax.sharding import PartitionSpec as P

MESH = pl.DeviceIdType.MESH
F32 = jnp.float32
BF16 = jnp.bfloat16
HIGHEST = lax.Precision.HIGHEST
LANES = 128
WIDE = 4
NT = (((1,), (1,)), ((), ()))


def dot(a, b):
    return jnp.dot(a, b, preferred_element_type=F32)


def dot_nt(a, b):
    return lax.dot_general(a, b, NT, preferred_element_type=F32)


def parts(value):
    high = value.astype(BF16).astype(F32)
    return high, value - high


def stack_rows(value):
    high, low = parts(value)
    pieces = [high, low, high]
    if value.shape[0] == 8:
        pieces.append(jnp.zeros_like(value))
    return jnp.concatenate(pieces, axis=0).astype(BF16)


def stack_columns(value):
    high, low = parts(value)
    pieces = [high, high, low]
    if value.shape[1] == 8:
        pieces.append(jnp.zeros_like(value))
    return jnp.concatenate(pieces, axis=1).astype(BF16)


def cycle(
    n_slab,
    n_cross,
    cap,
    rhs_hbm,
    class_hbm,
    perm_hbm,
    vol_hbm,
    side_hbm,
    couple_hbm,
    smooth_hbm,
    restrict_hbm,
    coarse_hbm,
    owner_hbm,
    local_hbm,
    sol_ref,
    res_ref,
    rhs_ref,
    class_ref,
    perm_ref,
    vol_ref,
    side_ref,
    couple_ref,
    smooth_ref,
    restrict_ref,
    coarse_ref,
    owner_ref,
    local_ref,
    rs,
    label,
    halo_label,
    fields,
    halos,
    start_field,
    fine_res,
    acc,
    gx0,
    gx1,
    gy0,
    gy1,
    blocks_f32,
    op_stack,
    smooth_stack,
    prolong_stack,
    coarse_stack,
    perm_b,
    perm_inv,
    weights,
    owner_hot,
    rank_b,
    packed,
    local_hot,
    mail,
    coarse_keep,
    coarse_field,
    halo_coarse,
    load_sem,
    halo_send,
    halo_recv,
    mail_send,
    mail_recv,
    all_here,
):
    s, c = lax.axis_index("slab"), lax.axis_index("cross")
    owners = n_slab * n_cross
    s_up, s_down = lax.rem(s + 1, n_slab), lax.rem(s + n_slab - 1, n_slab)
    c_up, c_down = lax.rem(c + 1, n_cross), lax.rem(c + n_cross - 1, n_cross)
    lane = lax.broadcasted_iota(jnp.int32, (8, LANES), 1)

    barrier = pltpu.get_barrier_semaphore()

    def greet_slab(off, carry):
        pl.semaphore_signal(
            barrier, inc=1, device_id=(lax.rem(s + off, n_slab), c), device_id_type=MESH
        )
        return carry

    def greet_cross(off, carry):
        pl.semaphore_signal(
            barrier, inc=1, device_id=(s, lax.rem(c + off, n_cross)), device_id_type=MESH
        )
        return carry

    lax.fori_loop(1, n_slab, greet_slab, 0)
    lax.fori_loop(1, n_cross, greet_cross, 0)

    loads = [
        pltpu.make_async_copy(source, target, load_sem.at[k])
        for k, (source, target) in enumerate(
            (
                (rhs_hbm, rhs_ref),
                (class_hbm, class_ref),
                (perm_hbm, perm_ref),
                (vol_hbm, vol_ref),
                (side_hbm, side_ref),
                (couple_hbm, couple_ref),
                (smooth_hbm, smooth_ref),
                (restrict_hbm, restrict_ref),
                (coarse_hbm, coarse_ref),
                (owner_hbm, owner_ref),
                (local_hbm, local_ref),
            )
        )
    ]
    for k in (0, 1, 2, 6):
        loads[k].start()
    for k in (0, 1, 2, 6):
        loads[k].wait()
    for k in (3, 4, 5, 7, 8, 9, 10):
        loads[k].start()

    for xy in range(WIDE * WIDE):
        x, y = xy // WIDE, xy % WIDE
        rs[x, y] = rhs_ref[pl.ds(xy, 64, stride=WIDE * WIDE), :]
        label[x, y] = jnp.broadcast_to(class_ref[xy : xy + 1, :], (8, LANES)).astype(F32)

    sent = []

    def drain():
        for finish in sent:
            finish()

    def halo_copies(source, target, turn):
        plan = (
            (source.at[0], 1, (s_down, c)),
            (source.at[WIDE - 1], 0, (s_up, c)),
            (source.at[:, 0], 3, (s, c_down)),
            (source.at[:, WIDE - 1], 2, (s, c_up)),
        )
        return [
            pltpu.make_async_remote_copy(
                src_ref=face,
                dst_ref=target.at[side],
                send_sem=halo_send.at[turn, side],
                recv_sem=halo_recv.at[turn, side],
                device_id=device,
                device_id_type=MESH,
            )
            for face, side, device in plan
        ]

    def send_halo(source, target, turn):
        for copy in halo_copies(source, target, turn):
            copy.start()
            sent.append(copy.wait_send)

    def await_halo(source, target, turn):
        for copy in halo_copies(source, target, turn):
            copy.wait_recv()

    def perm_of(kind):
        value = jnp.zeros_like(kind)
        for k in range(16):
            value = jnp.where(kind == float(k), perm_ref[k], value)
        return value

    def own_perm(x, carry):
        for y in range(WIDE):
            value = perm_of(label[x, y])
            perm_b[x, y] = value
            perm_inv[x, y] = 1.0 / value
        return carry

    lax.fori_loop(0, WIDE, own_perm, 0)

    for m in range(16):
        rows = slice(64 * m, 64 * m + 64)
        smooth_stack[rows, :] = stack_columns(smooth_ref[rows, :])

    def smoothed(values, labels, inverses):
        product = dot(smooth_stack[...], jnp.concatenate([stack_rows(v) for v in values], axis=1))
        results = []
        for i, (label, inverse) in enumerate(zip(labels, inverses)):
            columns = slice(i * LANES, (i + 1) * LANES)
            value = product[0:64, columns].reshape(8, 8, LANES)
            for k in range(1, 16):
                block = product[64 * k : 64 * k + 64, columns].reshape(8, 8, LANES)
                value = jnp.where((label == float(k))[None], block, value)
            results.append((value * inverse[None]).reshape(64, LANES))
        return results

    def label_of(x, y):
        return label[x, y]

    def first_sweep(step, carry):
        x = step * 3 % WIDE
        for half in range(2):
            ys = (2 * half, 2 * half + 1)
            found = smoothed(
                [rs[x, y] for y in ys],
                [label_of(x, y) for y in ys],
                [perm_inv[x, y] for y in ys],
            )
            for y, value in zip(ys, found):
                start_field[x, y] = value
        return carry

    first_sweep(0, 0)
    first_sweep(1, 0)
    pl.semaphore_wait(barrier, n_slab + n_cross - 2)
    send_halo(label, halo_label, 6)
    first_copies = halo_copies(start_field, halos.at[3], 0)
    first_copies[0].start()
    first_copies[1].start()
    first_sweep(2, 0)
    first_sweep(3, 0)
    first_copies[2].start()
    first_copies[3].start()
    sent.extend(copy.wait_send for copy in first_copies)
    for k in (3, 4, 5, 7, 8, 9, 10):
        loads[k].wait()

    def greet_again(off, carry):
        pl.semaphore_signal(
            all_here, inc=1, device_id=(lax.rem(s + off, n_slab), c), device_id_type=MESH
        )
        return carry

    lax.fori_loop(1, n_slab, greet_again, 0)

    blocks_f32[0:64, :] = vol_ref[...]
    blocks_f32[64:448, :] = side_ref[...]
    for m in range(3):
        plus = couple_ref[m * 64 : (m + 1) * 64, :]
        blocks_f32[448 + 128 * m : 512 + 128 * m, :] = plus.T
        blocks_f32[512 + 128 * m : 576 + 128 * m, :] = plus
    blocks_f32[832:896, :] = jnp.where(
        lax.broadcasted_iota(jnp.int32, (64, 64), 0) == lax.broadcasted_iota(jnp.int32, (64, 64), 1),
        1.0,
        0.0,
    )
    for m in range(13):
        rows = slice(64 * m, 64 * m + 64)
        op_stack[rows, :] = stack_columns(blocks_f32[rows, :])
    restrict = restrict_ref[...]
    short = lax.dot_general(
        blocks_f32[...], restrict, NT, precision=HIGHEST, preferred_element_type=F32
    )
    prolong_stack[...] = stack_columns(short)
    tiny = [
        jnp.dot(restrict, short[64 * m : 64 * m + 64], precision=HIGHEST, preferred_element_type=F32)
        for m in range(13)
    ]
    coarse_stack[...] = stack_columns(jnp.concatenate(tiny + [jnp.zeros((8, 8), F32)], axis=0))
    restrict_cols = stack_columns(jnp.concatenate([restrict, jnp.zeros_like(restrict)], axis=0))

    hot_rows = lax.broadcasted_iota(jnp.int32, (owners, LANES), 0)
    before = jnp.concatenate(
        [
            jnp.where(
                lax.broadcasted_iota(jnp.int32, (LANES, LANES), 0)
                < lax.broadcasted_iota(jnp.int32, (LANES, LANES), 1),
                1.0,
                0.0,
            ),
            jnp.ones((LANES, LANES), F32),
        ],
        axis=1,
    ).astype(BF16)
    seen = jnp.zeros((owners, LANES), F32)
    for xy in range(WIDE * WIDE):
        x, y = xy // WIDE, xy % WIDE
        hot = jnp.where(hot_rows == owner_ref[xy : xy + 1, :], 1.0, 0.0)
        hot_low = hot.astype(BF16)
        owner_hot[0:owners, xy * LANES : (xy + 1) * LANES] = hot_low
        owner_hot[owners : 2 * owners, xy * LANES : (xy + 1) * LANES] = hot_low
        counted = dot(hot_low, before)
        rank = jnp.sum(hot * (counted[:, 0:LANES] + seen), axis=0, keepdims=True)
        seen = seen + counted[:, LANES : 2 * LANES]
        rank_b[x, y] = jnp.broadcast_to(rank, (8, LANES))

    side_y = WIDE
    side_x = n_slab // side_y
    me = s * n_cross + c
    s_x, s_y = s // side_y, lax.rem(s, side_y)

    def hops(step):
        return min(step[0], side_x - step[0]) + min(step[1], side_y - step[1])

    far_first = sorted(
        ((i, j) for i in range(side_x) for j in range(side_y)), key=lambda step: -hops(step)
    )

    def post(turn):
        for step in far_first:
            to_slab = lax.rem(s_x + step[0], side_x) * side_y + lax.rem(s_y + step[1], side_y)

            def one(off, carry):
                to_cross = lax.rem(c + off, n_cross)
                pltpu.make_async_remote_copy(
                    src_ref=mail.at[turn, 0, to_slab * n_cross + to_cross],
                    dst_ref=mail.at[turn, 1, me],
                    send_sem=mail_send.at[turn],
                    recv_sem=mail_recv.at[turn],
                    device_id=(to_slab, to_cross),
                    device_id_type=MESH,
                ).start()
                return carry

            lax.fori_loop(0 if hops(step) else 1, n_cross, one, 0, unroll=True)
        sent.append(functools.partial(release, turn))
        mail[turn, 1, me] = mail[turn, 0, me]

    def collect(turn):
        part = mail.at[turn, 1, pl.ds(0, owners - 1)]
        pltpu.make_async_copy(part, part, mail_recv.at[turn]).wait()

    def release(turn):
        part = mail.at[turn, 0, pl.ds(0, owners - 1)]
        pltpu.make_async_copy(part, part, mail_send.at[turn]).wait()

    def write_mail(turn, value):
        mail[turn, 0] = value.reshape(owners, cap // 16, LANES)

    def read_mail(turn):
        return mail[turn, 1].reshape(owners, cap * 8).T

    def pack(load):
        def one(x, carry):
            for y in range(WIDE):
                rank = rank_b[x, y]
                keep = [rank == float(r) for r in range(cap)]
                columns = pl.ds(pl.multiple_of((x * WIDE + y) * LANES, LANES), LANES)
                for i, piece in enumerate(parts(load(x, y))):
                    spread = jnp.concatenate([jnp.where(k, piece, 0.0) for k in keep], axis=0)
                    packed[i * cap * 8 : (i + 1) * cap * 8, columns] = spread.astype(BF16)
            return carry

        for x in range(WIDE):
            one(x, 0)

    def to_owner_start(turn, load):
        pack(load)
        slots = dot_nt(owner_hot[0:owners, :], packed[...])
        write_mail(turn, slots[:, 0 : cap * 8] + slots[:, cap * 8 : 2 * cap * 8])
        post(turn)

    def to_owner_end(turn):
        collect(turn)
        return read_mail(turn)

    def gather_sum(arrived):
        flat = jnp.concatenate([arrived[8 * r : 8 * r + 8] for r in range(cap)], axis=1)
        high, low = parts(flat)
        both = dot_nt(jnp.concatenate([high, low], axis=0).astype(BF16), local_hot[...])
        return both[0:8] + both[8:16]

    def from_owner_start(turn, value):
        high, low = parts(value)
        both = dot(jnp.concatenate([high, low], axis=0).astype(BF16), local_hot[...])
        flat = both[0:8] + both[8:16]
        out = jnp.concatenate([flat[:, owners * r : owners * (r + 1)] for r in range(cap)], axis=0)
        write_mail(turn, out.T)
        post(turn)

    def from_owner_end(turn, target):
        collect(turn)
        high, low = parts(read_mail(turn))
        spread = jnp.concatenate([high, low], axis=1).astype(BF16)
        for pair in range(WIDE * WIDE // 2):
            both = dot(spread, owner_hot[:, pair * 2 * LANES : (pair + 1) * 2 * LANES])
            for i in range(2):
                x, y = (2 * pair + i) // WIDE, (2 * pair + i) % WIDE
                rank = rank_b[x, y]
                value = jnp.zeros((8, LANES), F32)
                for r in range(cap):
                    value = jnp.where(
                        rank == float(r),
                        both[8 * r : 8 * r + 8, i * LANES : (i + 1) * LANES],
                        value,
                    )
                coarse_field[target, x, y] = value

    def own_products(load, stack, rows, extra=None):
        def one(x, carry):
            for half in range(2):
                ys = (2 * half, 2 * half + 1)
                product = dot(stack[...], jnp.concatenate([load(x, y) for y in ys], axis=1))
                for i, y in enumerate(ys):

                    def block(b):
                        return product[b * rows : (b + 1) * rows, i * LANES : (i + 1) * LANES]

                    def scaled(weight, value):
                        return weight[None] * value.reshape(rows // 8, 8, LANES)

                    total = scaled(perm_b[x, y], block(0))
                    for d in range(6):
                        total = total + scaled(weights[d, x, y], block(1 + d))
                    total = total - scaled(weights[10, x, y], pltpu.roll(block(11), 1, 1))
                    total = total - scaled(weights[11, x, y], pltpu.roll(block(12), LANES - 1, 1))
                    acc[x, y, 0:rows, :] = total.reshape(rows, LANES)
                    gx0[x + 1, y, 0:rows, :] = block(7)
                    gx1[x, y, 0:rows, :] = block(8)
                    gy0[x, y + 1, 0:rows, :] = block(9)
                    gy1[x, y, 0:rows, :] = block(10)
                    if extra is not None:
                        extra(x, y, block(13))
            return carry

        for x in range(WIDE):
            one(x, 0)

    def halo_products(load, stack, rows):
        for side in range(4):
            data = jnp.concatenate([load(side, j) for j in range(WIDE)], axis=1)
            if rows == 64:
                product = dot(stack[(7 + side) * rows : (8 + side) * rows, :], data)
            else:
                product = dot(stack[...], data)[(7 + side) * rows : (8 + side) * rows]
            for j in range(WIDE):
                value = product[:, j * LANES : (j + 1) * LANES]
                if side == 0:
                    gx0[0, j, 0:rows, :] = value
                elif side == 1:
                    gx1[WIDE, j, 0:rows, :] = value
                elif side == 2:
                    gy0[j, 0, 0:rows, :] = value
                else:
                    gy1[j, WIDE, 0:rows, :] = value

    def applied(x, y, rows):
        def scaled(weight, value):
            return weight[None] * value.reshape(rows // 8, 8, LANES)

        total = acc[x, y, 0:rows, :].reshape(rows // 8, 8, LANES)
        total = total - scaled(weights[6, x, y], gx0[x, y, 0:rows, :])
        total = total - scaled(weights[7, x, y], gx1[x + 1, y, 0:rows, :])
        total = total - scaled(weights[8, x, y], gy0[x, y, 0:rows, :])
        total = total - scaled(weights[9, x, y], gy1[x, y + 1, 0:rows, :])
        return total.reshape(rows, LANES)

    await_halo(label, halo_label, 6)
    inside = (s > 0, s < n_slab - 1, c > 0, c < n_cross - 1)
    for side in range(4):
        for j in range(WIDE):
            halo_coarse[0, side, j] = perm_of(halo_label[side, j])

    for x in range(WIDE):
        for y in range(WIDE):
            own = perm_b[x, y]

            def rim(side, j):
                return jnp.where(inside[side], halo_coarse[0, side, j], 0.0)

            beside = (
                perm_b[x - 1, y] if x > 0 else rim(0, y),
                perm_b[x + 1, y] if x < WIDE - 1 else rim(1, y),
                perm_b[x, y - 1] if y > 0 else rim(2, x),
                perm_b[x, y + 1] if y < WIDE - 1 else rim(3, x),
                jnp.where(lane > 0, pltpu.roll(own, 1, 1), 0.0),
                jnp.where(lane < LANES - 1, pltpu.roll(own, LANES - 1, 1), 0.0),
            )
            there = (
                True if x > 0 else inside[0],
                True if x < WIDE - 1 else inside[1],
                True if y > 0 else inside[2],
                True if y < WIDE - 1 else inside[3],
                lane > 0,
                lane < LANES - 1,
            )
            for d in range(6):
                kn = beside[d]
                w = jnp.where(kn > 0.0, 2.0 * own * kn / (own + kn), 2.0 * own)
                weights[d, x, y] = w
                weights[6 + d, x, y] = w if there[d] is True else jnp.where(there[d], w, 0.0)

    def fine_stack(ref, *lead):
        return lambda x, y: stack_rows(ref[(*lead, x, y)])

    own_products(fine_stack(start_field), op_stack, 64)

    await_halo(start_field, halos.at[3], 0)
    halo_products(fine_stack(halos, 3), op_stack, 64)

    def sweep(residue, iterate, target, turn):
        copies = halo_copies(fields.at[target], halos.at[target], turn)
        for step, x in enumerate((0, WIDE - 1, 1, 2)):
            for half in range(2):
                ys = (2 * half, 2 * half + 1)
                found = smoothed(
                    [residue(x, y) for y in ys],
                    [label_of(x, y) for y in ys],
                    [perm_inv[x, y] for y in ys],
                )
                for y, value in zip(ys, found):
                    fields[target, x, y] = iterate(x, y) + value
            if step < 2:
                copies[step].start()
        copies[2].start()
        copies[3].start()
        sent.extend(copy.wait_send for copy in copies)

    sweep(
        lambda x, y: rs[x, y] - applied(x, y, 64), lambda x, y: start_field[x, y], 0, 1
    )
    own_products(fine_stack(fields, 0), op_stack, 64)

    def keys(x, y):
        row = lax.broadcasted_iota(jnp.int32, (8, LANES), 0)
        label = jnp.broadcast_to(local_ref[pl.ds(x * WIDE + y, 1), :], (8, LANES)).astype(F32) + 1.0
        return jnp.where(row == 0, label, jnp.where(row == 1, perm_b[x, y], 0.0))

    pl.semaphore_wait(all_here, n_slab - 1)
    to_owner_start(0, keys)

    await_halo(fields.at[0], halos.at[0], 1)
    halo_products(fine_stack(halos, 0), op_stack, 64)

    def second_residue(x, carry):
        rest = []
        for y in range(WIDE):
            value = rs[x, y] - applied(x, y, 64)
            fine_res[x, y] = value
            rest.append(stack_rows(value))
        found = dot(restrict_cols, jnp.concatenate(rest, axis=1))
        for y in range(WIDE):
            coarse_field[2, x, y] = found[0:8, y * LANES : (y + 1) * LANES]
        return carry

    for x in range(WIDE):
        second_residue(x, 0)

    def coarse_step(value):
        product = jnp.dot(
            coarse_ref[...], value, precision=HIGHEST, preferred_element_type=F32
        )
        return coarse_keep[0] * product

    to_owner_start(1, lambda x, y: coarse_field[2, x, y])
    arrived = to_owner_end(0)
    hot_ids = lax.broadcasted_iota(jnp.int32, (LANES, owners), 0).astype(F32) + 1.0
    for r in range(cap):
        local_hot[:, r * owners : (r + 1) * owners] = jnp.where(
            hot_ids == arrived[8 * r : 8 * r + 1, :], 1.0, 0.0
        ).astype(BF16)
    perm_sum = gather_sum(arrived)[1:2, :]
    coarse_keep[0] = jnp.broadcast_to(1.0 / (1.0 + perm_sum), (8, LANES))

    coarse_res = gather_sum(to_owner_end(1))
    first = coarse_step(coarse_res)
    from_owner_start(3, first)
    from_owner_end(3, 0)
    send_halo(coarse_field.at[0], halo_coarse.at[1], 2)
    own_products(fine_stack(coarse_field, 0), coarse_stack, 8)
    await_halo(coarse_field.at[0], halo_coarse.at[1], 2)
    halo_products(fine_stack(halo_coarse, 1), coarse_stack, 8)
    to_owner_start(2, lambda x, y: applied(x, y, 8))
    again = coarse_res - gather_sum(to_owner_end(2))
    second = first + coarse_step(again)
    from_owner_start(4, second)
    from_owner_end(4, 1)
    send_halo(coarse_field.at[1], halo_coarse.at[2], 3)

    def add_prolonged(x, y, value):
        fields[3, x, y] = fields[0, x, y] + value

    own_products(fine_stack(coarse_field, 1), prolong_stack, 64, add_prolonged)
    await_halo(coarse_field.at[1], halo_coarse.at[2], 3)
    halo_products(fine_stack(halo_coarse, 2), prolong_stack, 64)
    sweep(lambda x, y: fine_res[x, y] - applied(x, y, 64), lambda x, y: fields[3, x, y], 1, 4)

    own_products(fine_stack(fields, 1), op_stack, 64)
    await_halo(fields.at[1], halos.at[1], 4)
    halo_products(fine_stack(halos, 1), op_stack, 64)
    sweep(
        lambda x, y: rs[x, y] - applied(x, y, 64), lambda x, y: fields[1, x, y], 2, 5
    )
    own_products(fine_stack(fields, 2), op_stack, 64)
    for xy in range(WIDE * WIDE):
        sol_ref[pl.ds(xy, 64, stride=WIDE * WIDE), :] = fields[2, xy // WIDE, xy % WIDE]
    await_halo(fields.at[2], halos.at[2], 5)
    halo_products(fine_stack(halos, 2), op_stack, 64)
    for xy in range(WIDE * WIDE):
        x, y = xy // WIDE, xy % WIDE
        res_ref[pl.ds(xy, 64, stride=WIDE * WIDE), :] = rs[x, y] - applied(x, y, 64)

    drain()


def hand_over(sol_in, res_in, sol_out, res_out, sem):
    rows = sol_in.shape[0] // 4
    copies = [
        pltpu.make_async_copy(
            source.at[pl.ds(k * rows, rows)], target.at[pl.ds(k * rows, rows)], sem.at[i, k]
        )
        for i, (source, target) in enumerate(((sol_in, sol_out), (res_in, res_out)))
        for k in range(4)
    ]
    for copy in copies:
        copy.start()
    for copy in copies:
        copy.wait()


def local(
    n_slab,
    n_cross,
    cap,
    rhs,
    classes,
    perm,
    vol_block,
    side_blocks,
    couple,
    smoother_blocks,
    restrict_map,
    coarse_block,
    owners,
    agg_local,
):
    count = n_slab * n_cross
    face = (WIDE, WIDE)
    flat = jax.ShapeDtypeStruct((64 * WIDE * WIDE, LANES), F32)
    scratch = [
        pltpu.VMEM((64 * WIDE * WIDE, LANES), F32),
        pltpu.VMEM((WIDE * WIDE, LANES), jnp.int32),
        pltpu.SMEM((16,), F32),
        pltpu.VMEM((64, 64), F32),
        pltpu.VMEM((6 * 64, 64), F32),
        pltpu.VMEM((3 * 64, 64), F32),
        pltpu.VMEM((16 * 64, 64), F32),
        pltpu.VMEM((8, 64), F32),
        pltpu.VMEM((8, 8), F32),
        pltpu.VMEM((WIDE * WIDE, LANES), jnp.int32),
        pltpu.VMEM((WIDE * WIDE, LANES), jnp.int32),
        pltpu.VMEM((*face, 64, LANES), F32),
        pltpu.VMEM((*face, 8, LANES), F32),
        pltpu.VMEM((4, WIDE, 8, LANES), F32),
        pltpu.VMEM((4, *face, 64, LANES), F32),
        pltpu.VMEM((4, 4, WIDE, 64, LANES), F32),
        pltpu.VMEM((*face, 64, LANES), F32),
        pltpu.VMEM((*face, 64, LANES), F32),
        pltpu.VMEM((*face, 64, LANES), F32),
        pltpu.VMEM((WIDE + 1, WIDE, 64, LANES), F32),
        pltpu.VMEM((WIDE + 1, WIDE, 64, LANES), F32),
        pltpu.VMEM((WIDE, WIDE + 1, 64, LANES), F32),
        pltpu.VMEM((WIDE, WIDE + 1, 64, LANES), F32),
        pltpu.VMEM((14 * 64, 64), F32),
        pltpu.VMEM((13 * 64, 192), BF16),
        pltpu.VMEM((16 * 64, 192), BF16),
        pltpu.VMEM((14 * 64, 32), BF16),
        pltpu.VMEM((14 * 8, 32), BF16),
        pltpu.VMEM((*face, 8, LANES), F32),
        pltpu.VMEM((*face, 8, LANES), F32),
        pltpu.VMEM((12, *face, 8, LANES), F32),
        pltpu.VMEM((2 * count, WIDE * WIDE * LANES), BF16),
        pltpu.VMEM((*face, 8, LANES), F32),
        pltpu.VMEM((2 * cap * 8, WIDE * WIDE * LANES), BF16),
        pltpu.VMEM((LANES, cap * count), BF16),
        pltpu.VMEM((5, 2, count, cap // 16, LANES), F32),
        pltpu.VMEM((1, 8, LANES), F32),
        pltpu.VMEM((3, *face, 8, LANES), F32),
        pltpu.VMEM((3, 4, WIDE, 8, LANES), F32),
        pltpu.SemaphoreType.DMA((11,)),
        pltpu.SemaphoreType.DMA((7, 4)),
        pltpu.SemaphoreType.DMA((7, 4)),
        pltpu.SemaphoreType.DMA((5,)),
        pltpu.SemaphoreType.DMA((5,)),
        pltpu.SemaphoreType.REGULAR,
    ]
    flops = 2 * 2048 * (5 * 832 + 5 * 1024) * 192
    kept = pltpu.VMEM(flat.shape, F32)
    vmem = pl.BlockSpec(memory_space=pltpu.VMEM)
    arguments = (
        rhs.reshape(64 * WIDE * WIDE, LANES),
        classes.reshape(WIDE * WIDE, LANES),
        perm,
        vol_block,
        side_blocks.reshape(6 * 64, 64),
        couple.reshape(3 * 64, 64),
        smoother_blocks.reshape(16 * 64, 64),
        restrict_map,
        coarse_block,
        owners.reshape(WIDE * WIDE, LANES),
        agg_local.reshape(WIDE * WIDE, LANES),
    )
    solved, residue = pl.pallas_call(
        functools.partial(cycle, n_slab, n_cross, cap),
        out_shape=(kept, kept),
        in_specs=[pl.BlockSpec(memory_space=pltpu.HBM)] * 11,
        out_specs=(vmem, vmem),
        scratch_shapes=scratch,
        compiler_params=pltpu.CompilerParams(
            collective_id=0, has_side_effects=True, vmem_limit_bytes=40 * 1024 * 1024
        ),
        cost_estimate=pl.CostEstimate(flops=flops, bytes_accessed=4 << 20, transcendentals=0),
    )(*(pltpu.with_memory_space_constraint(value, pltpu.HBM) for value in arguments))
    solved, residue = pl.pallas_call(
        hand_over,
        out_shape=(pltpu.HBM(flat.shape, F32),) * 2,
        in_specs=[vmem, vmem],
        out_specs=(pl.BlockSpec(memory_space=pltpu.HBM),) * 2,
        scratch_shapes=[pltpu.SemaphoreType.DMA((2, 4))],
        compiler_params=pltpu.CompilerParams(vmem_limit_bytes=8 * 1024 * 1024),
    )(*(pltpu.with_memory_space_constraint(value, pltpu.VMEM) for value in (solved, residue)))
    return solved.reshape(rhs.shape), residue.reshape(rhs.shape)


def solution(mesh, cap=32):
    placed = (
        P(None, "slab", "cross", None),
        P("slab", "cross", None),
        P(),
        P(),
        P(),
        P(),
        P(),
        P(),
        P(),
        P("slab", "cross", None, None),
        P("slab", "cross", None),
    )
    return jax.shard_map(
        functools.partial(local, mesh.shape["slab"], mesh.shape["cross"], cap),
        mesh=mesh,
        in_specs=placed,
        out_specs=(P(None, "slab", "cross", None), P(None, "slab", "cross", None)),
        check_vma=False,
    )
```

```python
import functools

import jax
import jax.numpy as jnp
from jax import lax
from jax.experimental import pallas as pl
from jax.experimental.pallas import tpu as pltpu
from jax.sharding import PartitionSpec as P

MESH = pl.DeviceIdType.MESH
F32 = jnp.float32
BF16 = jnp.bfloat16
HIGHEST = lax.Precision.HIGHEST
LANES = 128
WIDE = 4
NT = (((1,), (1,)), ((), ()))


def dot(a, b):
    return jnp.dot(a, b, preferred_element_type=F32)


def dot_nt(a, b):
    return lax.dot_general(a, b, NT, preferred_element_type=F32)


def parts(value):
    high = value.astype(BF16).astype(F32)
    return high, value - high


def stack_rows(value):
    high, low = parts(value)
    pieces = [high, low, high]
    if value.shape[0] == 8:
        pieces.append(jnp.zeros_like(value))
    return jnp.concatenate(pieces, axis=0).astype(BF16)


def stack_columns(value):
    high, low = parts(value)
    pieces = [high, high, low]
    if value.shape[1] == 8:
        pieces.append(jnp.zeros_like(value))
    return jnp.concatenate(pieces, axis=1).astype(BF16)


def cycle(
    n_slab,
    n_cross,
    cap,
    rhs_hbm,
    class_hbm,
    perm_hbm,
    vol_hbm,
    side_hbm,
    couple_hbm,
    smooth_hbm,
    restrict_hbm,
    coarse_hbm,
    owner_hbm,
    local_hbm,
    sol_ref,
    res_ref,
    rhs_ref,
    class_ref,
    perm_ref,
    vol_ref,
    side_ref,
    couple_ref,
    smooth_ref,
    restrict_ref,
    coarse_ref,
    owner_ref,
    local_ref,
    rs,
    label,
    halo_label,
    fields,
    halos,
    start_field,
    fine_res,
    acc,
    gx0,
    gx1,
    gy0,
    gy1,
    blocks_f32,
    op_stack,
    smooth_stack,
    prolong_stack,
    coarse_stack,
    perm_b,
    perm_inv,
    weights,
    owner_hot,
    rank_b,
    packed,
    local_hot,
    mail,
    coarse_keep,
    coarse_field,
    halo_coarse,
    load_sem,
    halo_send,
    halo_recv,
    mail_send,
    mail_recv,
    all_here,
):
    s, c = lax.axis_index("slab"), lax.axis_index("cross")
    owners = n_slab * n_cross
    s_up, s_down = lax.rem(s + 1, n_slab), lax.rem(s + n_slab - 1, n_slab)
    c_up, c_down = lax.rem(c + 1, n_cross), lax.rem(c + n_cross - 1, n_cross)
    lane = lax.broadcasted_iota(jnp.int32, (8, LANES), 1)

    loads = [
        pltpu.make_async_copy(source, target, load_sem.at[k])
        for k, (source, target) in enumerate(
            (
                (rhs_hbm, rhs_ref),
                (class_hbm, class_ref),
                (perm_hbm, perm_ref),
                (vol_hbm, vol_ref),
                (side_hbm, side_ref),
                (couple_hbm, couple_ref),
                (smooth_hbm, smooth_ref),
                (restrict_hbm, restrict_ref),
                (coarse_hbm, coarse_ref),
                (owner_hbm, owner_ref),
                (local_hbm, local_ref),
            )
        )
    ]
    for k in (0, 1, 2, 6):
        loads[k].start()

    barrier = pltpu.get_barrier_semaphore()

    def greet_slab(off, carry):
        pl.semaphore_signal(
            barrier, inc=1, device_id=(lax.rem(s + off, n_slab), c), device_id_type=MESH
        )
        return carry

    def greet_cross(off, carry):
        pl.semaphore_signal(
            barrier, inc=1, device_id=(s, lax.rem(c + off, n_cross)), device_id_type=MESH
        )
        return carry

    lax.fori_loop(1, n_slab, greet_slab, 0)
    lax.fori_loop(1, n_cross, greet_cross, 0)

    for k in (0, 1, 2, 6):
        loads[k].wait()
    for k in (3, 4, 5, 7, 8, 9, 10):
        loads[k].start()

    for xy in range(WIDE * WIDE):
        x, y = xy // WIDE, xy % WIDE
        rs[x, y] = rhs_ref[pl.ds(xy, 64, stride=WIDE * WIDE), :]
        label[x, y] = jnp.broadcast_to(class_ref[xy : xy + 1, :], (8, LANES)).astype(F32)

    sent = []

    def drain():
        for finish in sent:
            finish()

    def halo_copies(source, target, turn):
        plan = (
            (source.at[0], 1, (s_down, c)),
            (source.at[WIDE - 1], 0, (s_up, c)),
            (source.at[:, 0], 3, (s, c_down)),
            (source.at[:, WIDE - 1], 2, (s, c_up)),
        )
        return [
            pltpu.make_async_remote_copy(
                src_ref=face,
                dst_ref=target.at[side],
                send_sem=halo_send.at[turn, side],
                recv_sem=halo_recv.at[turn, side],
                device_id=device,
                device_id_type=MESH,
            )
            for face, side, device in plan
        ]

    def send_halo(source, target, turn):
        for copy in halo_copies(source, target, turn):
            copy.start()
            sent.append(copy.wait_send)

    def await_halo(source, target, turn):
        for copy in halo_copies(source, target, turn):
            copy.wait_recv()

    def perm_of(kind):
        value = jnp.zeros_like(kind)
        for k in range(16):
            value = jnp.where(kind == float(k), perm_ref[k], value)
        return value

    def own_perm(x, carry):
        for y in range(WIDE):
            value = perm_of(label[x, y])
            perm_b[x, y] = value
            perm_inv[x, y] = 1.0 / value
        return carry

    lax.fori_loop(0, WIDE, own_perm, 0)

    for m in range(16):
        rows = slice(64 * m, 64 * m + 64)
        smooth_stack[rows, :] = stack_columns(smooth_ref[rows, :])

    def smoothed(values, labels, inverses):
        product = dot(smooth_stack[...], jnp.concatenate([stack_rows(v) for v in values], axis=1))
        results = []
        for i, (label, inverse) in enumerate(zip(labels, inverses)):
            columns = slice(i * LANES, (i + 1) * LANES)
            value = product[0:64, columns].reshape(8, 8, LANES)
            for k in range(1, 16):
                block = product[64 * k : 64 * k + 64, columns].reshape(8, 8, LANES)
                value = jnp.where((label == float(k))[None], block, value)
            results.append((value * inverse[None]).reshape(64, LANES))
        return results

    def label_of(x, y):
        return label[x, y]

    def first_sweep(step, carry):
        x = step * 3 % WIDE
        for half in range(2):
            ys = (2 * half, 2 * half + 1)
            found = smoothed(
                [rs[x, y] for y in ys],
                [label_of(x, y) for y in ys],
                [perm_inv[x, y] for y in ys],
            )
            for y, value in zip(ys, found):
                start_field[x, y] = value
        return carry

    first_sweep(0, 0)
    first_sweep(1, 0)
    pl.semaphore_wait(barrier, n_slab + n_cross - 2)
    send_halo(label, halo_label, 6)
    first_copies = halo_copies(start_field, halos.at[3], 0)
    first_copies[0].start()
    first_copies[1].start()
    first_sweep(2, 0)
    first_sweep(3, 0)
    first_copies[2].start()
    first_copies[3].start()
    sent.extend(copy.wait_send for copy in first_copies)
    for k in (3, 4, 5, 7, 8, 9, 10):
        loads[k].wait()

    def greet_again(off, carry):
        pl.semaphore_signal(
            all_here, inc=1, device_id=(lax.rem(s + off, n_slab), c), device_id_type=MESH
        )
        return carry

    lax.fori_loop(1, n_slab, greet_again, 0)

    blocks_f32[0:64, :] = vol_ref[...]
    blocks_f32[64:448, :] = side_ref[...]
    for m in range(3):
        plus = couple_ref[m * 64 : (m + 1) * 64, :]
        blocks_f32[448 + 128 * m : 512 + 128 * m, :] = plus.T
        blocks_f32[512 + 128 * m : 576 + 128 * m, :] = plus
    blocks_f32[832:896, :] = jnp.where(
        lax.broadcasted_iota(jnp.int32, (64, 64), 0) == lax.broadcasted_iota(jnp.int32, (64, 64), 1),
        1.0,
        0.0,
    )
    for m in range(13):
        rows = slice(64 * m, 64 * m + 64)
        op_stack[rows, :] = stack_columns(blocks_f32[rows, :])
    restrict = restrict_ref[...]
    scaled_restrict = jnp.dot(
        coarse_ref[...], restrict, precision=HIGHEST, preferred_element_type=F32
    )
    short = lax.dot_general(
        blocks_f32[...], restrict, NT, precision=HIGHEST, preferred_element_type=F32
    )
    prolong_stack[...] = stack_columns(short)
    tiny = [
        jnp.dot(
            scaled_restrict,
            short[64 * m : 64 * m + 64],
            precision=HIGHEST,
            preferred_element_type=F32,
        )
        for m in range(13)
    ]
    coarse_stack[...] = stack_columns(jnp.concatenate(tiny + [jnp.zeros((8, 8), F32)], axis=0))
    restrict_cols = stack_columns(
        jnp.concatenate([scaled_restrict, jnp.zeros_like(restrict)], axis=0)
    )

    hot_rows = lax.broadcasted_iota(jnp.int32, (owners, LANES), 0)
    before = jnp.concatenate(
        [
            jnp.where(
                lax.broadcasted_iota(jnp.int32, (LANES, LANES), 0)
                < lax.broadcasted_iota(jnp.int32, (LANES, LANES), 1),
                1.0,
                0.0,
            ),
            jnp.ones((LANES, LANES), F32),
        ],
        axis=1,
    ).astype(BF16)
    seen = jnp.zeros((owners, LANES), F32)
    for xy in range(WIDE * WIDE):
        x, y = xy // WIDE, xy % WIDE
        hot = jnp.where(hot_rows == owner_ref[xy : xy + 1, :], 1.0, 0.0)
        hot_low = hot.astype(BF16)
        owner_hot[0:owners, xy * LANES : (xy + 1) * LANES] = hot_low
        owner_hot[owners : 2 * owners, xy * LANES : (xy + 1) * LANES] = hot_low
        counted = dot(hot_low, before)
        rank = jnp.sum(hot * (counted[:, 0:LANES] + seen), axis=0, keepdims=True)
        seen = seen + counted[:, LANES : 2 * LANES]
        rank_b[x, y] = jnp.broadcast_to(rank, (8, LANES))

    side_y = WIDE
    side_x = n_slab // side_y
    me = s * n_cross + c
    s_x, s_y = s // side_y, lax.rem(s, side_y)

    def hops(step):
        return min(step[0], side_x - step[0]) + min(step[1], side_y - step[1])

    far_first = sorted(
        ((i, j) for i in range(side_x) for j in range(side_y)), key=lambda step: -hops(step)
    )

    def post(turn):
        for step in far_first:
            to_slab = lax.rem(s_x + step[0], side_x) * side_y + lax.rem(s_y + step[1], side_y)

            def one(off, carry):
                to_cross = lax.rem(c + off, n_cross)
                pltpu.make_async_remote_copy(
                    src_ref=mail.at[turn, 0, to_slab * n_cross + to_cross],
                    dst_ref=mail.at[turn, 1, me],
                    send_sem=mail_send.at[turn],
                    recv_sem=mail_recv.at[turn],
                    device_id=(to_slab, to_cross),
                    device_id_type=MESH,
                ).start()
                return carry

            offsets = sorted(range(n_cross), key=lambda off: abs(2 * off - n_cross))
            for off in offsets:
                if off or hops(step):
                    one(off, 0)
        sent.append(functools.partial(release, turn))
        mail[turn, 1, me] = mail[turn, 0, me]

    def collect(turn):
        part = mail.at[turn, 1, pl.ds(0, owners - 1)]
        pltpu.make_async_copy(part, part, mail_recv.at[turn]).wait()

    def release(turn):
        part = mail.at[turn, 0, pl.ds(0, owners - 1)]
        pltpu.make_async_copy(part, part, mail_send.at[turn]).wait()

    def write_mail(turn, value):
        mail[turn, 0] = value.reshape(owners, cap // 16, LANES)

    def read_mail(turn):
        return mail[turn, 1].reshape(owners, cap * 8).T

    def pack(load):
        def one(x, carry):
            for y in range(WIDE):
                rank = rank_b[x, y]
                keep = [rank == float(r) for r in range(cap)]
                columns = pl.ds(pl.multiple_of((x * WIDE + y) * LANES, LANES), LANES)
                for i, piece in enumerate(parts(load(x, y))):
                    spread = jnp.concatenate([jnp.where(k, piece, 0.0) for k in keep], axis=0)
                    packed[i * cap * 8 : (i + 1) * cap * 8, columns] = spread.astype(BF16)
            return carry

        for x in range(WIDE):
            one(x, 0)

    def to_owner_start(turn, load):
        pack(load)
        slots = dot_nt(owner_hot[0:owners, :], packed[...])
        write_mail(turn, slots[:, 0 : cap * 8] + slots[:, cap * 8 : 2 * cap * 8])
        post(turn)

    def to_owner_end(turn):
        collect(turn)
        return read_mail(turn)

    def gather_sum(arrived):
        flat = jnp.concatenate([arrived[8 * r : 8 * r + 8] for r in range(cap)], axis=1)
        high, low = parts(flat)
        both = dot_nt(jnp.concatenate([high, low], axis=0).astype(BF16), local_hot[...])
        return both[0:8] + both[8:16]

    def from_owner_start(turn, value):
        high, low = parts(value)
        both = dot(jnp.concatenate([high, low], axis=0).astype(BF16), local_hot[...])
        flat = both[0:8] + both[8:16]
        out = jnp.concatenate([flat[:, owners * r : owners * (r + 1)] for r in range(cap)], axis=0)
        write_mail(turn, out.T)
        post(turn)

    def from_owner_end(turn, target):
        collect(turn)
        high, low = parts(read_mail(turn))
        spread = jnp.concatenate([high, low], axis=1).astype(BF16)
        copies = halo_copies(coarse_field.at[target], halo_coarse.at[target + 1], target + 2)
        sent.extend(copy.wait_send for copy in copies)
        for pair in (0, 1, 6, 7, 2, 3, 4, 5):
            both = dot(spread, owner_hot[:, pair * 2 * LANES : (pair + 1) * 2 * LANES])
            for i in range(2):
                x, y = (2 * pair + i) // WIDE, (2 * pair + i) % WIDE
                rank = rank_b[x, y]
                value = jnp.zeros((8, LANES), F32)
                for r in range(cap):
                    value = jnp.where(
                        rank == float(r),
                        both[8 * r : 8 * r + 8, i * LANES : (i + 1) * LANES],
                        value,
                    )
                coarse_field[target, x, y] = value
            if pair in (1, 7):
                copies[pair // 7].start()
        copies[2].start()
        copies[3].start()

    def own_products(load, stack, rows, extra=None):
        def one(x, carry):
            for half in range(2):
                ys = (2 * half, 2 * half + 1)
                product = dot(stack[...], jnp.concatenate([load(x, y) for y in ys], axis=1))
                for i, y in enumerate(ys):

                    def block(b):
                        return product[b * rows : (b + 1) * rows, i * LANES : (i + 1) * LANES]

                    def scaled(weight, value):
                        return weight[None] * value.reshape(rows // 8, 8, LANES)

                    total = scaled(perm_b[x, y], block(0))
                    for d in range(6):
                        total = total + scaled(weights[d, x, y], block(1 + d))
                    total = total - scaled(weights[10, x, y], pltpu.roll(block(11), 1, 1))
                    total = total - scaled(weights[11, x, y], pltpu.roll(block(12), LANES - 1, 1))
                    acc[x, y, 0:rows, :] = total.reshape(rows, LANES)
                    gx0[x + 1, y, 0:rows, :] = block(7)
                    gx1[x, y, 0:rows, :] = block(8)
                    gy0[x, y + 1, 0:rows, :] = block(9)
                    gy1[x, y, 0:rows, :] = block(10)
                    if extra is not None:
                        extra(x, y, block(13))
            return carry

        for x in range(WIDE):
            one(x, 0)

    def halo_products(load, stack, rows):
        for side in range(4):
            data = jnp.concatenate([load(side, j) for j in range(WIDE)], axis=1)
            if rows == 64:
                product = dot(stack[(7 + side) * rows : (8 + side) * rows, :], data)
            else:
                product = dot(stack[...], data)[(7 + side) * rows : (8 + side) * rows]
            for j in range(WIDE):
                value = product[:, j * LANES : (j + 1) * LANES]
                if side == 0:
                    gx0[0, j, 0:rows, :] = value
                elif side == 1:
                    gx1[WIDE, j, 0:rows, :] = value
                elif side == 2:
                    gy0[j, 0, 0:rows, :] = value
                else:
                    gy1[j, WIDE, 0:rows, :] = value

    def applied(x, y, rows):
        def scaled(weight, value):
            return weight[None] * value.reshape(rows // 8, 8, LANES)

        total = acc[x, y, 0:rows, :].reshape(rows // 8, 8, LANES)
        total = total - scaled(weights[6, x, y], gx0[x, y, 0:rows, :])
        total = total - scaled(weights[7, x, y], gx1[x + 1, y, 0:rows, :])
        total = total - scaled(weights[8, x, y], gy0[x, y, 0:rows, :])
        total = total - scaled(weights[9, x, y], gy1[x, y + 1, 0:rows, :])
        return total.reshape(rows, LANES)

    await_halo(label, halo_label, 6)
    inside = (s > 0, s < n_slab - 1, c > 0, c < n_cross - 1)
    for side in range(4):
        for j in range(WIDE):
            halo_coarse[0, side, j] = perm_of(halo_label[side, j])

    for x in range(WIDE):
        for y in range(WIDE):
            own = perm_b[x, y]

            def rim(side, j):
                return jnp.where(inside[side], halo_coarse[0, side, j], 0.0)

            beside = (
                perm_b[x - 1, y] if x > 0 else rim(0, y),
                perm_b[x + 1, y] if x < WIDE - 1 else rim(1, y),
                perm_b[x, y - 1] if y > 0 else rim(2, x),
                perm_b[x, y + 1] if y < WIDE - 1 else rim(3, x),
                jnp.where(lane > 0, pltpu.roll(own, 1, 1), 0.0),
                jnp.where(lane < LANES - 1, pltpu.roll(own, LANES - 1, 1), 0.0),
            )
            there = (
                True if x > 0 else inside[0],
                True if x < WIDE - 1 else inside[1],
                True if y > 0 else inside[2],
                True if y < WIDE - 1 else inside[3],
                lane > 0,
                lane < LANES - 1,
            )
            for d in range(6):
                kn = beside[d]
                w = jnp.where(kn > 0.0, 2.0 * own * kn / (own + kn), 2.0 * own)
                weights[d, x, y] = w
                weights[6 + d, x, y] = w if there[d] is True else jnp.where(there[d], w, 0.0)

    def fine_stack(ref, *lead):
        return lambda x, y: stack_rows(ref[(*lead, x, y)])

    own_products(fine_stack(start_field), op_stack, 64)

    await_halo(start_field, halos.at[3], 0)
    halo_products(fine_stack(halos, 3), op_stack, 64)

    def sweep(residue, iterate, target, turn):
        copies = halo_copies(fields.at[target], halos.at[target], turn)
        for step, x in enumerate((0, WIDE - 1, 1, 2)):
            for half in range(2):
                ys = (2 * half, 2 * half + 1)
                found = smoothed(
                    [residue(x, y) for y in ys],
                    [label_of(x, y) for y in ys],
                    [perm_inv[x, y] for y in ys],
                )
                for y, value in zip(ys, found):
                    fields[target, x, y] = iterate(x, y) + value
            if step < 2:
                copies[step].start()
        copies[2].start()
        copies[3].start()
        sent.extend(copy.wait_send for copy in copies)

    sweep(
        lambda x, y: rs[x, y] - applied(x, y, 64), lambda x, y: start_field[x, y], 0, 1
    )
    own_products(fine_stack(fields, 0), op_stack, 64)

    def keys(x, y):
        row = lax.broadcasted_iota(jnp.int32, (8, LANES), 0)
        label = jnp.broadcast_to(local_ref[pl.ds(x * WIDE + y, 1), :], (8, LANES)).astype(F32) + 1.0
        return jnp.where(row == 0, label, jnp.where(row == 1, perm_b[x, y], 0.0))

    pl.semaphore_wait(all_here, n_slab - 1)
    to_owner_start(0, keys)

    await_halo(fields.at[0], halos.at[0], 1)
    halo_products(fine_stack(halos, 0), op_stack, 64)

    def second_residue(x, carry):
        rest = []
        for y in range(WIDE):
            value = rs[x, y] - applied(x, y, 64)
            fine_res[x, y] = value
            rest.append(stack_rows(value))
        found = dot(restrict_cols, jnp.concatenate(rest, axis=1))
        for y in range(WIDE):
            coarse_field[2, x, y] = found[0:8, y * LANES : (y + 1) * LANES]
        return carry

    for x in range(WIDE):
        second_residue(x, 0)

    def coarse_step(value):
        return coarse_keep[0] * value

    to_owner_start(1, lambda x, y: coarse_field[2, x, y])
    arrived = to_owner_end(0)
    hot_ids = lax.broadcasted_iota(jnp.int32, (LANES, owners), 0).astype(F32) + 1.0
    for r in range(cap):
        local_hot[:, r * owners : (r + 1) * owners] = jnp.where(
            hot_ids == arrived[8 * r : 8 * r + 1, :], 1.0, 0.0
        ).astype(BF16)
    perm_sum = gather_sum(arrived)[1:2, :]
    coarse_keep[0] = jnp.broadcast_to(1.0 / (1.0 + perm_sum), (8, LANES))

    coarse_res = gather_sum(to_owner_end(1))
    first = coarse_step(coarse_res)
    from_owner_start(3, first)
    from_owner_end(3, 0)
    own_products(fine_stack(coarse_field, 0), coarse_stack, 8)
    await_halo(coarse_field.at[0], halo_coarse.at[1], 2)
    halo_products(fine_stack(halo_coarse, 1), coarse_stack, 8)
    to_owner_start(2, lambda x, y: applied(x, y, 8))
    again = coarse_res - gather_sum(to_owner_end(2))
    second = first + coarse_step(again)
    from_owner_start(4, second)
    from_owner_end(4, 1)

    def add_prolonged(x, y, value):
        fields[3, x, y] = fields[0, x, y] + value

    own_products(fine_stack(coarse_field, 1), prolong_stack, 64, add_prolonged)
    await_halo(coarse_field.at[1], halo_coarse.at[2], 3)
    halo_products(fine_stack(halo_coarse, 2), prolong_stack, 64)
    sweep(lambda x, y: fine_res[x, y] - applied(x, y, 64), lambda x, y: fields[3, x, y], 1, 4)

    own_products(fine_stack(fields, 1), op_stack, 64)
    await_halo(fields.at[1], halos.at[1], 4)
    halo_products(fine_stack(halos, 1), op_stack, 64)
    sweep(
        lambda x, y: rs[x, y] - applied(x, y, 64), lambda x, y: fields[1, x, y], 2, 5
    )
    own_products(fine_stack(fields, 2), op_stack, 64)
    for xy in range(WIDE * WIDE):
        sol_ref[pl.ds(xy, 64, stride=WIDE * WIDE), :] = fields[2, xy // WIDE, xy % WIDE]
    await_halo(fields.at[2], halos.at[2], 5)
    halo_products(fine_stack(halos, 2), op_stack, 64)
    for xy in range(WIDE * WIDE):
        x, y = xy // WIDE, xy % WIDE
        res_ref[pl.ds(xy, 64, stride=WIDE * WIDE), :] = rs[x, y] - applied(x, y, 64)

    drain()


def hand_over(sol_in, res_in, sol_out, res_out, sem):
    rows = sol_in.shape[0] // 4
    copies = [
        pltpu.make_async_copy(
            source.at[pl.ds(k * rows, rows)], target.at[pl.ds(k * rows, rows)], sem.at[i, k]
        )
        for i, (source, target) in enumerate(((sol_in, sol_out), (res_in, res_out)))
        for k in range(4)
    ]
    for copy in copies:
        copy.start()
    for copy in copies:
        copy.wait()


def local(
    n_slab,
    n_cross,
    cap,
    rhs,
    classes,
    perm,
    vol_block,
    side_blocks,
    couple,
    smoother_blocks,
    restrict_map,
    coarse_block,
    owners,
    agg_local,
):
    count = n_slab * n_cross
    face = (WIDE, WIDE)
    flat = jax.ShapeDtypeStruct((64 * WIDE * WIDE, LANES), F32)
    scratch = [
        pltpu.VMEM((64 * WIDE * WIDE, LANES), F32),
        pltpu.VMEM((WIDE * WIDE, LANES), jnp.int32),
        pltpu.SMEM((16,), F32),
        pltpu.VMEM((64, 64), F32),
        pltpu.VMEM((6 * 64, 64), F32),
        pltpu.VMEM((3 * 64, 64), F32),
        pltpu.VMEM((16 * 64, 64), F32),
        pltpu.VMEM((8, 64), F32),
        pltpu.VMEM((8, 8), F32),
        pltpu.VMEM((WIDE * WIDE, LANES), jnp.int32),
        pltpu.VMEM((WIDE * WIDE, LANES), jnp.int32),
        pltpu.VMEM((*face, 64, LANES), F32),
        pltpu.VMEM((*face, 8, LANES), F32),
        pltpu.VMEM((4, WIDE, 8, LANES), F32),
        pltpu.VMEM((4, *face, 64, LANES), F32),
        pltpu.VMEM((4, 4, WIDE, 64, LANES), F32),
        pltpu.VMEM((*face, 64, LANES), F32),
        pltpu.VMEM((*face, 64, LANES), F32),
        pltpu.VMEM((*face, 64, LANES), F32),
        pltpu.VMEM((WIDE + 1, WIDE, 64, LANES), F32),
        pltpu.VMEM((WIDE + 1, WIDE, 64, LANES), F32),
        pltpu.VMEM((WIDE, WIDE + 1, 64, LANES), F32),
        pltpu.VMEM((WIDE, WIDE + 1, 64, LANES), F32),
        pltpu.VMEM((14 * 64, 64), F32),
        pltpu.VMEM((13 * 64, 192), BF16),
        pltpu.VMEM((16 * 64, 192), BF16),
        pltpu.VMEM((14 * 64, 32), BF16),
        pltpu.VMEM((14 * 8, 32), BF16),
        pltpu.VMEM((*face, 8, LANES), F32),
        pltpu.VMEM((*face, 8, LANES), F32),
        pltpu.VMEM((12, *face, 8, LANES), F32),
        pltpu.VMEM((2 * count, WIDE * WIDE * LANES), BF16),
        pltpu.VMEM((*face, 8, LANES), F32),
        pltpu.VMEM((2 * cap * 8, WIDE * WIDE * LANES), BF16),
        pltpu.VMEM((LANES, cap * count), BF16),
        pltpu.VMEM((5, 2, count, cap // 16, LANES), F32),
        pltpu.VMEM((1, 8, LANES), F32),
        pltpu.VMEM((3, *face, 8, LANES), F32),
        pltpu.VMEM((3, 4, WIDE, 8, LANES), F32),
        pltpu.SemaphoreType.DMA((11,)),
        pltpu.SemaphoreType.DMA((7, 4)),
        pltpu.SemaphoreType.DMA((7, 4)),
        pltpu.SemaphoreType.DMA((5,)),
        pltpu.SemaphoreType.DMA((5,)),
        pltpu.SemaphoreType.REGULAR,
    ]
    flops = 2 * 2048 * (5 * 832 + 5 * 1024) * 192
    kept = pltpu.VMEM(flat.shape, F32)
    vmem = pl.BlockSpec(memory_space=pltpu.VMEM)
    arguments = (
        rhs.reshape(64 * WIDE * WIDE, LANES),
        classes.reshape(WIDE * WIDE, LANES),
        perm,
        vol_block,
        side_blocks.reshape(6 * 64, 64),
        couple.reshape(3 * 64, 64),
        smoother_blocks.reshape(16 * 64, 64),
        restrict_map,
        coarse_block,
        owners.reshape(WIDE * WIDE, LANES),
        agg_local.reshape(WIDE * WIDE, LANES),
    )
    solved, residue = pl.pallas_call(
        functools.partial(cycle, n_slab, n_cross, cap),
        out_shape=(kept, kept),
        in_specs=[pl.BlockSpec(memory_space=pltpu.HBM)] * 11,
        out_specs=(vmem, vmem),
        scratch_shapes=scratch,
        compiler_params=pltpu.CompilerParams(
            collective_id=0, has_side_effects=True, vmem_limit_bytes=40 * 1024 * 1024
        ),
        cost_estimate=pl.CostEstimate(flops=flops, bytes_accessed=4 << 20, transcendentals=0),
    )(*(pltpu.with_memory_space_constraint(value, pltpu.HBM) for value in arguments))
    solved, residue = pl.pallas_call(
        hand_over,
        out_shape=(pltpu.HBM(flat.shape, F32),) * 2,
        in_specs=[vmem, vmem],
        out_specs=(pl.BlockSpec(memory_space=pltpu.HBM),) * 2,
        scratch_shapes=[pltpu.SemaphoreType.DMA((2, 4))],
        compiler_params=pltpu.CompilerParams(vmem_limit_bytes=8 * 1024 * 1024),
    )(*(pltpu.with_memory_space_constraint(value, pltpu.VMEM) for value in (solved, residue)))
    return solved.reshape(rhs.shape), residue.reshape(rhs.shape)


def solution(mesh, cap=32):
    placed = (
        P(None, "slab", "cross", None),
        P("slab", "cross", None),
        P(),
        P(),
        P(),
        P(),
        P(),
        P(),
        P(),
        P("slab", "cross", None, None),
        P("slab", "cross", None),
    )
    return jax.shard_map(
        functools.partial(local, mesh.shape["slab"], mesh.shape["cross"], cap),
        mesh=mesh,
        in_specs=placed,
        out_specs=(P(None, "slab", "cross", None), P(None, "slab", "cross", None)),
        check_vma=False,
    )
```
